32 devices in a mesh: groups: 2 (over y), tm: 4 (over z), head: 4 (over x, core).
Axes of the slice: x: 2, y: 2, z: 4, core: 2. Of those that a mesh axis runs over, the one named last changes fastest.
Arguments:
- queries: bfloat16 [3072, 24, 128], P(('groups', 'tm'), 'head'), parts along dimension 0, may hold values from -6 to 6
- key_rows: bfloat16 [3072, 24, 128], P(('groups', 'tm'), 'head'), parts along dimension 0, may hold values from -6 to 6
- value_rows: bfloat16 [3072, 24, 128], P(('groups', 'tm'), 'head'), parts along dimension 0, may hold values from -6 to 6
- keep_tiles: int32 [24, 9], P(('groups', 'tm')), parts along dimension 0, may hold values from 0 to 1, as said below
- out_weight: bfloat16 [3072, 5120], P('head', 'tm'), may hold values from -0.109375 to 0.109375
- gate_scale: float32 [10240], P(('groups', 'head')), parts along dimension 0, may hold values from 1 to 3
Outputs:
- gated_branch: bfloat16 [3072, 5120], P(('groups', 'tm'), 'head'), parts along dimension 0
The draws below stay inside these ranges and needn't reach their ends.
There are 2 independent parts, one for each index of `groups`. The reference program is written for one: setup_inputs(seed, part) draws one part's arguments, and reference() takes and returns one part's arrays. A program takes and returns all parts, laid end to end along the dimension named above; an argument that names none is the same for every part. Nothing has to cross between parts.
Inputs may be any that keep to these rules, and one draw needn't show every extreme that they name: `keep_tiles`: each row is one query tile; the query tile itself is always kept; each row keeps 3 to 6 tiles, and some row keeps exactly 6.
All inputs are finite; a program needn't handle non-finite values.
Results may differ from the reference program's by a relative error of at most 0.014.
Values may be sent and summed in bfloat16 or wider, within the bound.
No kernel may reach another device: no remote copies, remote signals or barrier semaphores. Data moves between devices by JAX's collectives and lax.ppermute only.
A program may use at most 64 MiB of HBM per device.

```python
import math
import jax
import jax.numpy as jnp
from jax import lax

D = 5120
HEADS = 24
HD = 128
TILE = 128
TILES_DEV = 3
KEEP_MIN = 3
KEEP_MAX = 6
TOK_DEV = 384
TOKENS = 1536
TILES = 12
REACH = 1
CAND = 9
N_TM = 4
N_HEAD = 4


def shared_rows(key, which):
    shape = (TOKENS, HEADS, HD)
    base = jax.random.normal(jax.random.fold_in(key, 11 + which), shape, jnp.float32) * 1.5
    return jnp.clip(base, -6.0, 6.0)


def draw_queries(key, part):
    return shared_rows(key, 0).astype(jnp.bfloat16)


def draw_key_rows(key, part):
    return shared_rows(key, 1).astype(jnp.bfloat16)


def draw_keep_tiles(key, part):
    counts = jax.random.randint(jax.random.fold_in(key, 1), (TILES,), KEEP_MIN, KEEP_MAX + 1)
    special = jax.random.randint(jax.random.fold_in(key, 2), (), 0, TILES)
    row_ids = jnp.arange(TILES, dtype=jnp.int32)
    counts = jnp.where(row_ids == special, KEEP_MAX, counts)
    row_keys = jax.random.split(jax.random.fold_in(key, 3), TILES)
    ranking = jax.vmap(lambda row_key: jax.random.permutation(row_key, CAND))(row_keys).astype(jnp.int32)
    own_index = REACH * TILES_DEV + row_ids % TILES_DEV
    cand_ids = jnp.arange(CAND, dtype=jnp.int32)
    own_rank = jnp.sum(jnp.where(cand_ids[None, :] == own_index[:, None], ranking, 0), axis=1)
    other_rank = ranking - (ranking > own_rank[:, None]).astype(jnp.int32)
    is_own = cand_ids[None, :] == own_index[:, None]
    kept = is_own | ~is_own & (other_rank < counts[:, None] - 1)
    return kept.astype(jnp.int32)


def shard_levels(rng, extent, cuts, smallest, top_value):
    gain, own = 1.0, jax.random.fold_in(rng, 6)
    for position, shards_of in cuts:
        heights = jnp.exp(jax.random.uniform(jax.random.fold_in(own, position), (shards_of,), jnp.float32, smallest / len(cuts), top_value / len(cuts)))
        gain = gain * jnp.repeat(heights, extent[position] // shards_of).reshape([-1 if axis == position else 1 for axis in range(len(extent))])
    return gain


def centred(rng, shape, scale, limit, pieces=(), kind=jnp.bfloat16):
    level = shard_levels(rng, shape, pieces, -0.22, 0.18) if pieces else 1.0
    values = jax.random.normal(rng, shape, jnp.float32) * scale * level
    return jnp.minimum(jnp.maximum(values, -limit), limit).astype(kind)


def setup_inputs(seed: int = 0, part: int = 0) -> dict:
    streams_of = jax.random.split(jax.random.key(seed), 7)
    own_keys = jax.random.split(jax.random.fold_in(streams_of[6], part), 7)
    queries = draw_queries(jax.random.fold_in(jax.random.fold_in(streams_of[6], part), 71), part)
    key_rows = draw_key_rows(jax.random.fold_in(jax.random.fold_in(streams_of[6], part), 71), part)
    value_rows = centred(own_keys[2], (TOKENS, HEADS, HD), 1.0, 6.0, ((0, 4), (1, 4)))
    keep_tiles = draw_keep_tiles(jax.random.fold_in(jax.random.fold_in(streams_of[6], part), 71), part)
    out_weight = centred(streams_of[4], (HEADS * HD, D), (HEADS * HD) ** -0.5, 0.109375, ((0, 4), (1, 4)))
    gate_scale = jnp.clip(1.0 + 2.0 * jax.random.uniform(own_keys[5], (D,), jnp.float32) ** shard_levels(own_keys[5], (D,), ((0, 4),), -0.2, 0.2), 1.0, 3.0)
    return {"queries": queries, "key_rows": key_rows, "value_rows": value_rows, "keep_tiles": keep_tiles, "out_weight": out_weight, "gate_scale": gate_scale}


def expand_mask(keep_rows, tile_len):
    tile_count, cand_count = keep_rows.shape
    wide = jnp.broadcast_to(keep_rows[:, None, :, None], (tile_count, tile_len, cand_count, tile_len))
    return wide.reshape(tile_count * tile_len, cand_count * tile_len)

def softmax_attend(query_block, key_block, value_block, allowed):
    score_scale = 1.0 / math.sqrt(HD)
    scores = jnp.einsum('qhd,khd->hqk', query_block.astype(jnp.float32), key_block.astype(jnp.float32)) * score_scale
    scores = jnp.where(allowed[None] > 0, scores, -jnp.inf)
    row_peak = lax.optimization_barrier(jnp.max(scores, axis=-1, keepdims=True))
    exp_scores = jnp.exp(scores - row_peak)
    row_total = lax.optimization_barrier(jnp.sum(exp_scores, axis=-1, keepdims=True))
    weights = (exp_scores / row_total).astype(jnp.bfloat16)
    attended = jnp.einsum('hqk,khd->qhd', weights.astype(jnp.float32), value_block.astype(jnp.float32))
    return attended.astype(jnp.bfloat16)

def reference(queries, key_rows, value_rows, keep_tiles, out_weight, gate_scale):
    slab_queries = queries.reshape(N_TM, TOK_DEV, HEADS, HD)
    slab_keys = key_rows.reshape(N_TM, TOK_DEV, HEADS, HD)
    slab_values = value_rows.reshape(N_TM, TOK_DEV, HEADS, HD)
    keep_slabs = keep_tiles.reshape(N_TM, TILES_DEV, CAND)
    offsets = jnp.arange(-REACH, REACH + 1, dtype=jnp.int32)

    def one_slab(slab_index):
        order = ((slab_index + offsets) % N_TM).astype(jnp.int32)
        cand_keys = jnp.take(slab_keys, order, axis=0).reshape(CAND * TILE, HEADS, HD)
        cand_values = jnp.take(slab_values, order, axis=0).reshape(CAND * TILE, HEADS, HD)
        allowed = expand_mask(keep_slabs[slab_index], TILE)
        return softmax_attend(slab_queries[slab_index], cand_keys, cand_values, allowed)
    attended = lax.map(one_slab, jnp.arange(N_TM, dtype=jnp.int32)).reshape(TOKENS, HEADS * HD)
    group_rows = HEADS * HD // N_HEAD
    projected = jnp.zeros((TOKENS, D), jnp.float32)
    for group_index in range(N_HEAD):
        lower_row = group_index * group_rows
        group_term = jnp.dot(attended[:, lower_row:lower_row + group_rows], out_weight[lower_row:lower_row + group_rows], preferred_element_type=jnp.float32)
        projected = projected + lax.optimization_barrier(group_term.astype(jnp.bfloat16)).astype(jnp.float32)
    return (gate_scale[None, :] * projected).astype(jnp.bfloat16)
```

```python
import math

import jax
import jax.numpy as jnp
from jax import lax
from jax.sharding import PartitionSpec as P

HD = 128
TILE = 128
KEEP_MAX = 6


def passed_along(array, axis, by):
    count = lax.axis_size(axis)
    return lax.ppermute(array, axis, [(i, (i + by) % count) for i in range(count)])


def swapped(array, axis, mask):
    count = lax.axis_size(axis)
    return lax.ppermute(array, axis, [(i, i ^ mask) for i in range(count)])


def compact_attend(queries, key_all, value_all, keep_tiles):
    tile_count, cand_count = keep_tiles.shape
    head_count = queries.shape[1]
    position = jnp.cumsum(keep_tiles, axis=1) - 1
    slot_ids = jnp.arange(KEEP_MAX, dtype=jnp.int32)
    selector = (
        (keep_tiles[:, None, :] > 0) & (position[:, None, :] == slot_ids[None, :, None])
    ).astype(jnp.int32)
    cand_ids = jnp.arange(cand_count, dtype=jnp.int32)
    chosen_index = jnp.sum(selector * cand_ids[None, None, :], axis=2)
    slot_valid = jnp.sum(selector, axis=2)
    key_tiles = key_all.reshape(cand_count, TILE, head_count, HD)
    value_tiles = value_all.reshape(cand_count, TILE, head_count, HD)
    chosen_keys = jnp.take(key_tiles, chosen_index, axis=0)
    chosen_values = jnp.take(value_tiles, chosen_index, axis=0)
    query_tiles = queries.reshape(tile_count, TILE, head_count, HD)
    score_scale = 1.0 / math.sqrt(HD)
    scores = (
        jnp.einsum(
            "tqhd,tskhd->thqsk", query_tiles, chosen_keys, preferred_element_type=jnp.float32
        )
        * score_scale
    )
    allowed = slot_valid[:, None, None, :, None] > 0
    scores = jnp.where(allowed, scores, -jnp.inf)
    row_peak = jnp.max(scores, axis=(3, 4), keepdims=True)
    exp_scores = jnp.exp(scores - row_peak)
    row_total = jnp.sum(exp_scores, axis=(3, 4), keepdims=True)
    weights = (exp_scores / row_total).astype(jnp.bfloat16)
    attended = jnp.einsum(
        "thqsk,tskhd->tqhd", weights, chosen_values, preferred_element_type=jnp.float32
    )
    return attended.astype(jnp.bfloat16).reshape(tile_count * TILE, head_count * HD)


def halo(key_rows, value_rows):
    reach_slabs = min(2, (lax.axis_size("tm") - 1) // 2)
    lower_list = []
    upper_list = []
    for distance in range(1, reach_slabs + 1):
        lower_list.append([passed_along(rows, "tm", distance) for rows in (key_rows, value_rows)])
        upper_list.append([passed_along(rows, "tm", -distance) for rows in (key_rows, value_rows)])
    return lower_list[::-1], upper_list


def joined(lower, own, upper):
    ordered = lower + [own] + upper
    return [jnp.concatenate([slab[which] for slab in ordered], axis=0) for which in (0, 1)]


def any_mesh(queries, key_rows, value_rows, keep_tiles, out_weight, gate_scale):
    lower, upper = halo(key_rows, value_rows)
    key_all, value_all = joined(lower, (key_rows, value_rows), upper)
    attended = compact_attend(queries, key_all, value_all, keep_tiles)
    partial_value = jnp.dot(
        attended,
        lax.all_gather(out_weight, "tm", axis=1, tiled=True),
        preferred_element_type=jnp.float32,
    )
    summed = lax.psum_scatter(
        partial_value.astype(jnp.bfloat16), "head", scatter_dimension=1, tiled=True
    ).astype(jnp.float32)
    return (gate_scale[None, :] * summed).astype(jnp.bfloat16)


def term(attended, weight):
    return jnp.dot(attended, weight, preferred_element_type=jnp.float32).astype(jnp.bfloat16)


def f32(array):
    return array.astype(jnp.float32)


def square_mesh(queries, key_rows, value_rows, keep_tiles, out_weight, gate_scale):
    video = lax.axis_index("groups")
    slab = lax.axis_index("tm")
    head = lax.axis_index("head")
    width = out_weight.shape[1] // 2

    lower, upper = halo(key_rows, value_rows)
    near = lax.dynamic_slice_in_dim(out_weight, video * width, width, 1)
    far = lax.dynamic_slice_in_dim(out_weight, (1 - video) * width, width, 1)
    near_2 = swapped(near, "tm", 2)
    near_1 = swapped(near, "tm", 1)
    near_3 = swapped(near_2, "tm", 1)
    far_1 = swapped(near_1, "groups", 1)
    far_2 = swapped(near_2, "groups", 1)
    far_3 = swapped(near_3, "groups", 1)

    key_all, value_all = joined(lower, (key_rows, value_rows), upper)
    attended = compact_attend(queries, key_all, value_all, keep_tiles)

    places = [(t, h) for t in range(4) for h in range(4)]
    same_core = slab % 2 == head % 2
    same_side = slab // 2 == head // 2

    def summed_pair(first, second, flip):
        kept = f32(jnp.where(same_core, first, second))
        given = jnp.where(same_core, second, first)
        total = kept + f32(swapped(given, "head", 1))
        pairs = [
            (4 * t + h, 4 * t + (h ^ 2)) for t, h in places if (t // 2 == h // 2) == flip
        ]
        return total, f32(lax.ppermute(total.astype(jnp.bfloat16), ("tm", "head"), pairs))

    own_near, own_far = summed_pair(term(attended, near), term(attended, near_1), False), summed_pair(
        term(attended, far), term(attended, far_1), False
    )
    other_near = summed_pair(term(attended, near_2), term(attended, near_3), True)
    other_far = summed_pair(term(attended, far_2), term(attended, far_3), True)
    halves = [
        jnp.where(same_side, own[0] + own[1], other[0] + other[1])
        for own, other in ((own_near, other_near), (own_far, other_far))
    ]
    ordered = [jnp.where(video == i, halves[0], halves[1]) for i in (0, 1)]
    projected = jnp.concatenate(ordered, axis=1)
    return (gate_scale[None, :] * projected).astype(jnp.bfloat16)


def solution(mesh):
    placed = (
        P(("groups", "tm"), "head", None),
        P(("groups", "tm"), "head", None),
        P(("groups", "tm"), "head", None),
        P(("groups", "tm"), None),
        P("head", "tm"),
        P(("groups", "head")),
    )
    sizes = (mesh.shape["groups"], mesh.shape["tm"], mesh.shape["head"])
    return jax.shard_map(
        square_mesh if sizes == (2, 4, 4) else any_mesh,
        mesh=mesh,
        in_specs=placed,
        out_specs=P(("groups", "tm"), "head"),
        check_vma=False,
    )
```

```python
import functools
import math

import jax
import jax.numpy as jnp
from jax import lax
from jax.experimental import pallas as pl
from jax.experimental.pallas import tpu as pltpu
from jax.sharding import PartitionSpec as P

TILE = 128
CUT = 256


def passed_along(array, axis, by):
    count = lax.axis_size(axis)
    return lax.ppermute(array, axis, [(i, (i + by) % count) for i in range(count)])


def swapped(array, axis, mask):
    count = lax.axis_size(axis)
    return lax.ppermute(array, axis, [(i, i ^ mask) for i in range(count)])


def attend_kernel(reach, score_scale, keep_ref, queries_ref, *refs):
    key_refs, value_refs, out_ref = refs[: 2 * reach + 1], refs[2 * reach + 1 : -1], refs[-1]
    tiles = queries_ref.shape[1] // TILE
    scale = score_scale * math.log2(math.e)
    for tile in range(tiles):
        query_tile = queries_ref[0, tile * TILE : (tile + 1) * TILE]
        scores = []
        for slab, key_ref in enumerate(key_refs):
            raw = lax.dot_general(
                query_tile, key_ref[0], (((1,), (1,)), ((), ())), preferred_element_type=jnp.float32
            )
            keep = keep_ref[tile : tile + 1, slab * tiles * TILE : (slab + 1) * tiles * TILE]
            scores.append(jnp.where(keep > 0, raw, -jnp.inf))
        peak = scores[0].max(axis=1, keepdims=True)
        for block in scores[1:]:
            peak = jnp.maximum(peak, block.max(axis=1, keepdims=True))
        total, out = 0.0, 0.0
        for block, value_ref in zip(scores, value_refs):
            weights = jnp.exp2((block - peak) * scale)
            total = total + weights.sum(axis=1, keepdims=True)
            out = out + jnp.dot(
                weights.astype(jnp.bfloat16), value_ref[0], preferred_element_type=jnp.float32
            )
        out_ref[tile * TILE : (tile + 1) * TILE] = (out / total).astype(out_ref.dtype)


def attend(queries, key_slabs, value_slabs, keep_tiles):
    rows, head_count, depth = queries.shape
    by_head = [rows_of.transpose(1, 0, 2) for rows_of in (queries, *key_slabs, *value_slabs)]
    keep = jnp.repeat(keep_tiles.astype(jnp.float32), TILE, axis=1)
    block = pl.BlockSpec((1, rows, depth), lambda head: (head, 0, 0))
    return pl.pallas_call(
        functools.partial(attend_kernel, len(key_slabs) // 2, 1.0 / math.sqrt(depth)),
        grid=(head_count,),
        out_shape=jax.ShapeDtypeStruct((rows, head_count * depth), jnp.bfloat16),
        in_specs=[pl.BlockSpec(keep.shape, lambda head: (0, 0))] + [block] * len(by_head),
        out_specs=pl.BlockSpec((rows, depth), lambda head: (0, head)),
        compiler_params=pltpu.CompilerParams(vmem_limit_bytes=32 * 2**20),
        cost_estimate=pl.CostEstimate(flops=2 * 10**10, bytes_accessed=10**7, transcendentals=0),
        name="attend",
    )(keep, *by_head)


def halo(key_rows, value_rows):
    reach_slabs = min(2, (lax.axis_size("tm") - 1) // 2)
    lower_list = []
    upper_list = []
    for distance in range(1, reach_slabs + 1):
        lower_list.append([passed_along(rows, "tm", distance) for rows in (key_rows, value_rows)])
        upper_list.append([passed_along(rows, "tm", -distance) for rows in (key_rows, value_rows)])
    return lower_list[::-1], upper_list


def all_slabs(lower, own, upper):
    ordered = lower + [own] + upper
    return [[slab[which] for slab in ordered] for which in (0, 1)]


def any_mesh(queries, key_rows, value_rows, keep_tiles, out_weight, gate_scale):
    lower, upper = halo(key_rows, value_rows)
    key_slabs, value_slabs = all_slabs(lower, (key_rows, value_rows), upper)
    attended = attend(queries, key_slabs, value_slabs, keep_tiles)
    partial_value = jnp.dot(
        attended,
        lax.all_gather(out_weight, "tm", axis=1, tiled=True),
        preferred_element_type=jnp.float32,
    )
    summed = lax.psum_scatter(
        partial_value.astype(jnp.bfloat16), "head", scatter_dimension=1, tiled=True
    ).astype(jnp.float32)
    return (gate_scale[None, :] * summed).astype(jnp.bfloat16)


def after(array, *others):
    return lax.optimization_barrier((array, *others))[0]


def f32(array):
    return array.astype(jnp.float32)


SMEM = pl.BlockSpec(memory_space=pltpu.SMEM)
WHOLE = pl.BlockSpec(memory_space=pltpu.VMEM)
LATER = pl.BlockSpec(memory_space=pl.ANY)


def local_call(kernel, outs, flags, arrays, earlier, name, flops=0):
    def body(*refs):
        count = len(flags) + len(arrays)
        kernel(*refs[:count], *refs[count + len(earlier) :])

    moved = sum(array.size * array.dtype.itemsize for array in (*arrays, *outs))
    return pl.pallas_call(
        body,
        out_shape=outs,
        in_specs=[SMEM] * len(flags) + [WHOLE] * len(arrays) + [LATER] * len(earlier),
        out_specs=[WHOLE] * len(outs),
        compiler_params=pltpu.CompilerParams(vmem_limit_bytes=40 * 2**20),
        cost_estimate=pl.CostEstimate(flops=flops, bytes_accessed=moved, transcendentals=0),
        name=name,
    )(*[jnp.int32(flag).reshape(1) for flag in flags], *arrays, *earlier)


def terms(mine, other, blocks, earlier=()):
    rows, depth = mine.shape
    width = sum(part.shape[1] for part in blocks[0])
    weights = [part for block in blocks for part in block]

    def kernel(mine_ref, other_ref, *refs):
        weight_refs, out_ref = list(refs[:-1]), refs[-1]
        for index, block in enumerate(blocks):
            column = 0
            for part in block:
                weight_ref = weight_refs.pop(0)
                columns = slice(column, column + part.shape[1])
                for video, rows_ref in enumerate((mine_ref, other_ref)):
                    out_ref[index, video, :, columns] = jnp.dot(
                        rows_ref[...], weight_ref[...], preferred_element_type=jnp.float32
                    ).astype(out_ref.dtype)
                column += part.shape[1]

    out = jax.ShapeDtypeStruct((len(blocks), 2, rows, width), jnp.bfloat16)
    flops = 4 * rows * depth * width * len(blocks) * 100
    return local_call(kernel, [out], (), (mine, other, *weights), earlier, "terms", flops)[0]


def add_cores(pair, arrived, first, earlier=()):
    def kernel(first_ref, pair_ref, arrived_ref, kept_ref, given_ref):
        for index, out_ref in ((1 - first_ref[0], kept_ref), (first_ref[0], given_ref)):
            total = f32(pair_ref[index]) + f32(arrived_ref[index])
            out_ref[...] = total.astype(out_ref.dtype)

    outs = [jax.ShapeDtypeStruct(pair.shape[1:], kind) for kind in (jnp.float32, jnp.bfloat16)]
    return local_call(kernel, outs, (first,), (pair, arrived), earlier, "add_cores")


def add_chips(kept, arrived, earlier=()):
    def kernel(kept_ref, arrived_ref, near_ref, far_ref):
        near_ref[...] = kept_ref[0] + f32(arrived_ref[0])
        far_ref[...] = (kept_ref[1] + f32(arrived_ref[1])).astype(far_ref.dtype)

    outs = [jax.ShapeDtypeStruct(kept.shape[1:], kind) for kind in (jnp.float32, jnp.bfloat16)]
    return local_call(kernel, outs, (), (kept, arrived), earlier, "add_chips")


def gated(gate_scale, units, which, video):
    rows = units[0][0][0].shape[0]
    width = sum(near.shape[1] for near, _ in units[0])
    counts = [len(unit) for unit in units]

    def kernel(which_ref, video_ref, gate_ref, *refs):
        part_refs, out_ref = list(refs[:-1]), refs[-1]
        for unit, count in enumerate(counts):
            own = [(part_refs.pop(0), part_refs.pop(0)) for _ in range(count)]
            for place in (0, 1):

                @pl.when((which_ref[0] == unit) & (video_ref[0] == place))
                def _():
                    column = 0
                    for pair in own:
                        for side, part_ref in enumerate(pair):
                            start = (side ^ place) * width + column
                            columns = slice(start, start + part_ref.shape[1])
                            out_ref[:, columns] = (
                                gate_ref[:, columns] * f32(part_ref[...])
                            ).astype(out_ref.dtype)
                        column += pair[0].shape[1]

    parts = [array for unit in units for pair in unit for array in pair]
    out = jax.ShapeDtypeStruct((rows, 2 * width), jnp.bfloat16)
    arrays = (gate_scale.reshape(1, -1), *parts)
    return local_call(kernel, [out], (which, video), arrays, (), "gated")[0]


def square_mesh(queries, key_rows, value_rows, keep_tiles, out_weight, gate_scale):
    video = lax.axis_index("groups")
    slab = lax.axis_index("tm")
    head = lax.axis_index("head")
    width = out_weight.shape[1] // 2
    cut = width - CUT

    lower, upper = halo(key_rows, value_rows)
    block_0 = [
        lax.dynamic_slice_in_dim(out_weight, video * width + start, size, 1)
        for start, size in ((0, cut), (cut, width - cut))
    ]
    early, late = lax.optimization_barrier((*block_0, lower, upper))[:2]
    block_2 = [swapped(early, "tm", 2)]
    block_1 = [swapped(early, "tm", 1)]

    key_slabs, value_slabs = all_slabs(lower, (key_rows, value_rows), upper)
    mine = attend(queries, key_slabs, value_slabs, keep_tiles)
    mine, late, block_2[0], block_1[0] = lax.optimization_barrier(
        (mine, late, block_2[0], block_1[0])
    )
    other = swapped(mine, "groups", 1)
    block_2.append(swapped(late, "tm", 2))
    block_1.append(swapped(late, "tm", 1))
    block_3 = [swapped(block, "tm", 1) for block in block_2]

    places = [(g, t, h) for g in range(2) for t in range(4) for h in range(4)]
    same_side = slab // 2 == head // 2

    def sent(array, group_mask, head_mask, flip):
        pairs = [
            (16 * g + 4 * t + h, 16 * (g ^ group_mask) + 4 * t + (h ^ head_mask))
            for g, t, h in places
            if (t % 2 == h % 2) != flip
        ]
        return lax.ppermute(array, ("groups", "tm", "head"), pairs)

    terms_1 = terms(mine, other, [block_0, block_2], [block_3[0]])
    kept_1, given_1 = add_cores(terms_1, sent(terms_1, 0, 1, True), same_side)
    across_1 = sent(given_1, 0, 2, False)
    terms_2 = terms(mine, other, [[block_1[0]], [block_3[0]]], [])
    near_1, far_1 = add_chips(kept_1, across_1)
    kept_2, given_2 = add_cores(terms_2, sent(terms_2, 0, 1, False), same_side)
    across_2 = sent(given_2, 0, 2, True)
    terms_3 = terms(mine, other, [[block_1[1]], [block_3[1]]], [])
    far_1 = sent(far_1, 1, 0, False)
    kept_3, given_3 = add_cores(terms_3, sent(terms_3, 0, 1, False), same_side, [far_1])
    across_3 = sent(given_3, 0, 2, True)
    near_2, far_2 = add_chips(kept_2, across_2)
    near_3, far_3 = add_chips(kept_3, across_3, [far_1, far_2])
    far_2 = sent(far_2, 1, 0, True)
    far_3 = sent(far_3, 1, 0, True)
    units = [[(near_1, far_1)], [(near_2, far_2), (near_3, far_3)]]
    return gated(gate_scale, units, (slab ^ head) & 1, video)


def solution(mesh):
    placed = (
        P(("groups", "tm"), "head", None),
        P(("groups", "tm"), "head", None),
        P(("groups", "tm"), "head", None),
        P(("groups", "tm"), None),
        P("head", "tm"),
        P(("groups", "head")),
    )
    sizes = (mesh.shape["groups"], mesh.shape["tm"], mesh.shape["head"])
    return jax.shard_map(
        square_mesh if sizes == (2, 4, 4) else any_mesh,
        mesh=mesh,
        in_specs=placed,
        out_specs=P(("groups", "tm"), "head"),
        check_vma=False,
    )
```

```python
import functools
import math

import jax
import jax.numpy as jnp
from jax import lax
from jax.experimental import pallas as pl
from jax.experimental.pallas import tpu as pltpu
from jax.sharding import PartitionSpec as P

TILE = 128
CUT = 256


def passed_along(array, axis, by):
    count = lax.axis_size(axis)
    return lax.ppermute(array, axis, [(i, (i + by) % count) for i in range(count)])


def swapped(array, axis, mask):
    count = lax.axis_size(axis)
    return lax.ppermute(array, axis, [(i, i ^ mask) for i in range(count)])


def attend_kernel(reach, score_scale, keep_ref, queries_ref, *refs):
    key_refs, value_refs, out_ref = refs[: 2 * reach + 1], refs[2 * reach + 1 : -1], refs[-1]
    tiles = queries_ref.shape[1] // TILE
    scale = score_scale * math.log2(math.e)
    for tile in range(tiles):
        query_tile = queries_ref[0, tile * TILE : (tile + 1) * TILE]
        scores = []
        for slab, key_ref in enumerate(key_refs):
            raw = lax.dot_general(
                query_tile, key_ref[0], (((1,), (1,)), ((), ())), preferred_element_type=jnp.float32
            )
            keep = keep_ref[tile : tile + 1, slab * tiles * TILE : (slab + 1) * tiles * TILE]
            scores.append(jnp.where(keep > 0, raw, -jnp.inf))
        peak = scores[0].max(axis=1, keepdims=True)
        for block in scores[1:]:
            peak = jnp.maximum(peak, block.max(axis=1, keepdims=True))
        total, out = 0.0, 0.0
        for block, value_ref in zip(scores, value_refs):
            weights = jnp.exp2((block - peak) * scale)
            total = total + weights.sum(axis=1, keepdims=True)
            out = out + jnp.dot(
                weights.astype(jnp.bfloat16), value_ref[0], preferred_element_type=jnp.float32
            )
        out_ref[tile * TILE : (tile + 1) * TILE] = (out / total).astype(out_ref.dtype)


def attend(queries, key_slabs, value_slabs, keep_tiles):
    rows, head_count, depth = queries.shape
    by_head = [rows_of.transpose(1, 0, 2) for rows_of in (queries, *key_slabs, *value_slabs)]
    keep = jnp.repeat(keep_tiles.astype(jnp.float32), TILE, axis=1)
    block = pl.BlockSpec((1, rows, depth), lambda head: (head, 0, 0))
    return pl.pallas_call(
        functools.partial(attend_kernel, len(key_slabs) // 2, 1.0 / math.sqrt(depth)),
        grid=(head_count,),
        out_shape=jax.ShapeDtypeStruct((rows, head_count * depth), jnp.bfloat16),
        in_specs=[pl.BlockSpec(keep.shape, lambda head: (0, 0))] + [block] * len(by_head),
        out_specs=pl.BlockSpec((rows, depth), lambda head: (0, head)),
        compiler_params=pltpu.CompilerParams(vmem_limit_bytes=16 * 2**20),
        cost_estimate=pl.CostEstimate(flops=2 * 10**10, bytes_accessed=10**7, transcendentals=0),
        name="attend",
    )(keep, *by_head)


def halo(key_rows, value_rows):
    reach_slabs = min(2, (lax.axis_size("tm") - 1) // 2)
    lower_list = []
    upper_list = []
    for distance in range(1, reach_slabs + 1):
        lower_list.append([passed_along(rows, "tm", distance) for rows in (key_rows, value_rows)])
        upper_list.append([passed_along(rows, "tm", -distance) for rows in (key_rows, value_rows)])
    return lower_list[::-1], upper_list


def diagonal(array):
    pairs = [(4 * g + h, 4 * (g ^ 1) + (h ^ 2)) for g in range(2) for h in range(4)]
    return lax.ppermute(array, ("groups", "head"), pairs)


def all_slabs(lower, own, upper):
    ordered = lower + [own] + upper
    return [[slab[which] for slab in ordered] for which in (0, 1)]


def any_mesh(queries, key_rows, value_rows, keep_tiles, out_weight, gate_scale):
    lower, upper = halo(key_rows, value_rows)
    key_slabs, value_slabs = all_slabs(lower, (key_rows, value_rows), upper)
    attended = attend(queries, key_slabs, value_slabs, keep_tiles)
    partial_value = jnp.dot(
        attended,
        lax.all_gather(out_weight, "tm", axis=1, tiled=True),
        preferred_element_type=jnp.float32,
    )
    summed = lax.psum_scatter(
        partial_value.astype(jnp.bfloat16), "head", scatter_dimension=1, tiled=True
    ).astype(jnp.float32)
    return (gate_scale[None, :] * summed).astype(jnp.bfloat16)


def after(array, *others):
    return lax.optimization_barrier((array, *others))[0]


def f32(array):
    return array.astype(jnp.float32)


SMEM = pl.BlockSpec(memory_space=pltpu.SMEM)
WHOLE = pl.BlockSpec(memory_space=pltpu.VMEM)
LATER = pl.BlockSpec(memory_space=pl.ANY)


def local_call(kernel, outs, flags, arrays, earlier, name, flops=0, left=(), scratch=()):
    def body(*refs):
        count = len(flags) + len(arrays) + len(left)
        kernel(*refs[:count], *refs[count + len(earlier) :])

    moved = sum(array.size * array.dtype.itemsize for array in (*arrays, *left, *outs))
    return pl.pallas_call(
        body,
        out_shape=outs,
        in_specs=[SMEM] * len(flags)
        + [WHOLE] * len(arrays)
        + [LATER] * (len(left) + len(earlier)),
        out_specs=[WHOLE] * len(outs),
        scratch_shapes=scratch,
        compiler_params=pltpu.CompilerParams(vmem_limit_bytes=16 * 2**20),
        cost_estimate=pl.CostEstimate(flops=flops, bytes_accessed=moved, transcendentals=0),
        name=name,
    )(*[jnp.int32(flag).reshape(1) for flag in flags], *arrays, *left, *earlier)


def terms(rows_of, blocks, role, first, cost, earlier=()):
    rows, depth = rows_of[0][0].shape
    width = blocks[0].shape[2]
    flat = [array for core in rows_of for array in core]

    def kernel(role_ref, first_ref, *refs):
        rows_refs, block_refs = refs[:4], refs[4:8]
        near_ref, far_ref, near_given_ref, far_given_ref, held_rows, weight, landed = refs[8:]
        out_refs = ((near_ref, far_ref), (near_given_ref, far_given_ref))

        def write(odd, second):
            copies = [
                pltpu.make_async_copy(
                    rows_ref,
                    held_rows.at[pl.ds(index % 2 * rows, rows), pl.ds(index // 2 * depth, depth)],
                    landed.at[index],
                )
                for index, rows_ref in enumerate(rows_refs)
            ] + [
                pltpu.make_async_copy(
                    block_refs[odd + 2 * (slot ^ second)].at[core],
                    weight.at[slot, pl.ds(core * depth, depth)],
                    landed.at[4 + 2 * slot + core],
                )
                for slot in (0, 1)
                for core in (0, 1)
            ]
            for copy in copies[6:] + copies[:6]:
                copy.start()
            for copy in copies[6:] + copies[:4]:
                copy.wait()
            for slot in (1, 0):
                if slot == 0:
                    for copy in copies[4:6]:
                        copy.wait()
                total = jnp.dot(
                    held_rows[...], weight[slot], preferred_element_type=jnp.float32
                )
                for video, out_ref in enumerate(out_refs[slot]):
                    out_ref[...] = total[video * rows : (video + 1) * rows].astype(out_ref.dtype)

        for odd in (0, 1):
            for second in (0, 1):
                chosen = (role_ref[0] == odd) & (first_ref[0] == 1 - second)
                pl.when(chosen)(functools.partial(write, odd, second))

    kinds = (jnp.float32, jnp.bfloat16, jnp.bfloat16, jnp.bfloat16)
    outs = [jax.ShapeDtypeStruct((rows, width), kind) for kind in kinds]
    scratch = [
        pltpu.VMEM((2 * rows, 2 * depth), jnp.bfloat16),
        pltpu.VMEM((2, 2 * depth, width), jnp.bfloat16),
        pltpu.SemaphoreType.DMA((8,)),
    ]
    left = (*flat, *blocks)
    return local_call(
        kernel, outs, (role, first), (), earlier, "terms", cost, left=left, scratch=scratch
    )


def held(arrays, earlier, cost=0):
    return pl.pallas_call(
        lambda *refs: None,
        out_shape=[jax.ShapeDtypeStruct(array.shape, array.dtype) for array in arrays],
        in_specs=[LATER] * (len(arrays) + len(earlier)),
        out_specs=[LATER] * len(arrays),
        input_output_aliases={index: index for index in range(len(arrays))},
        cost_estimate=pl.CostEstimate(flops=cost, bytes_accessed=0, transcendentals=0),
        name="held",
    )(*arrays, *earlier)


def gated(gate_scale, parts, video, earlier=()):
    rows = parts[0][0][0].shape[0]
    width = sum(near[0].shape[1] for near, _ in parts)

    def kernel(video_ref, gate_ref, *refs):
        out_ref = refs[-1]

        def write(place):
            part_refs = list(refs[:-1])
            column = 0
            for part in parts:
                for side, half in enumerate(part):
                    total = f32(part_refs.pop(0)[...])
                    for _ in half[1:]:
                        total = total + f32(part_refs.pop(0)[...])
                    start = (side ^ place) * width + column
                    columns = slice(start, start + total.shape[1])
                    out_ref[:, columns] = (gate_ref[:, columns] * total).astype(out_ref.dtype)
                column += part[0][0].shape[1]

        for place in (0, 1):
            pl.when(video_ref[0] == place)(functools.partial(write, place))

    arrays = [array for part in parts for half in part for array in half]
    out = jax.ShapeDtypeStruct((rows, 2 * width), jnp.bfloat16)
    arrays = (gate_scale.reshape(1, -1), *arrays)
    return local_call(kernel, [out], (video,), arrays, earlier, "gated")[0]


def square_mesh(queries, key_rows, value_rows, keep_tiles, out_weight, gate_scale):
    video = lax.axis_index("groups")
    slab = lax.axis_index("tm")
    head = lax.axis_index("head")
    width = out_weight.shape[1] // 2
    cut = width - CUT
    role = (slab ^ head) & 1
    first = slab // 2 == head // 2

    def passed(array, slab_mask, head_mask, odd):
        pairs = [
            (4 * t + h, 4 * (t ^ slab_mask) + (h ^ head_mask))
            for t in range(4)
            for h in range(4)
            if (t ^ h) & 1 == odd
        ]
        return lax.ppermute(array, ("tm", "head"), pairs)

    lower, upper = halo(key_rows, value_rows)
    half = lax.dynamic_slice_in_dim(out_weight, video * width, width, 1)
    both = jnp.stack([half, passed(half, 0, 1, 1)])
    early, late = lax.optimization_barrier((both[..., :cut], both[..., cut:], lower, upper))[:2]
    block_0 = [early, late]
    block_2 = [passed(early, 2, 0, 0)]
    block_1 = [passed(early, 1, 0, 0)]

    key_slabs, value_slabs = all_slabs(lower, (key_rows, value_rows), upper)
    mine = attend(queries, key_slabs, value_slabs, keep_tiles)
    mine, late, block_2[0], block_1[0] = lax.optimization_barrier(
        (mine, late, block_2[0], block_1[0])
    )
    other = swapped(mine, "groups", 1)
    rows_of = (mine, other), (swapped(mine, "head", 1), swapped(other, "head", 1))
    block_2 += held([passed(late, 2, 0, 0)], [], 100 * 2**33)
    late = held([late], [block_2[1]])[0]
    block_0[1] = late
    block_1.append(passed(late, 1, 0, 0))
    block_3 = [passed(block, 1, 0, 0) for block in block_2]
    parts = list(zip(block_0, block_1, block_2, block_3))

    cost = 100 * 2**33
    summed = []
    for part in parts:
        near, far, near_given, far_given = terms(rows_of, part, role, first, cost)
        across = swapped(near_given, "head", 2)
        summed.append(((near, across), (swapped(far, "groups", 1), diagonal(far_given))))
    return gated(gate_scale, summed, video)


def solution(mesh):
    placed = (
        P(("groups", "tm"), "head", None),
        P(("groups", "tm"), "head", None),
        P(("groups", "tm"), "head", None),
        P(("groups", "tm"), None),
        P("head", "tm"),
        P(("groups", "head")),
    )
    sizes = (mesh.shape["groups"], mesh.shape["tm"], mesh.shape["head"])
    return jax.shard_map(
        square_mesh if sizes == (2, 4, 4) else any_mesh,
        mesh=mesh,
        in_specs=placed,
        out_specs=P(("groups", "tm"), "head"),
        check_vma=False,
    )
```

```python
import functools
import math

import jax
import jax.numpy as jnp
from jax import lax
from jax.experimental import pallas as pl
from jax.experimental.pallas import tpu as pltpu
from jax.sharding import PartitionSpec as P

TILE = 128
CUT = 256


def passed_along(array, axis, by):
    count = lax.axis_size(axis)
    return lax.ppermute(array, axis, [(i, (i + by) % count) for i in range(count)])


def swapped(array, axis, mask):
    count = lax.axis_size(axis)
    return lax.ppermute(array, axis, [(i, i ^ mask) for i in range(count)])


def attend_kernel(reach, score_scale, keep_ref, queries_ref, *refs):
    key_refs, value_refs, out_ref = refs[: 2 * reach + 1], refs[2 * reach + 1 : -1], refs[-1]
    tiles = queries_ref.shape[1] // TILE
    scale = score_scale * math.log2(math.e)
    for tile in range(tiles):
        query_tile = queries_ref[0, tile * TILE : (tile + 1) * TILE]
        scores = []
        for slab, key_ref in enumerate(key_refs):
            raw = lax.dot_general(
                query_tile, key_ref[0], (((1,), (1,)), ((), ())), preferred_element_type=jnp.float32
            )
            keep = keep_ref[tile : tile + 1, slab * tiles * TILE : (slab + 1) * tiles * TILE]
            scores.append(jnp.where(keep > 0, raw, -jnp.inf))
        peak = scores[0].max(axis=1, keepdims=True)
        for block in scores[1:]:
            peak = jnp.maximum(peak, block.max(axis=1, keepdims=True))
        total, out = 0.0, 0.0
        for block, value_ref in zip(scores, value_refs):
            weights = jnp.exp2((block - peak) * scale)
            total = total + weights.sum(axis=1, keepdims=True)
            out = out + jnp.dot(
                weights.astype(jnp.bfloat16), value_ref[0], preferred_element_type=jnp.float32
            )
        out_ref[tile * TILE : (tile + 1) * TILE] = (out / total).astype(out_ref.dtype)


def attend(queries, key_slabs, value_slabs, keep_tiles):
    rows, head_count, depth = queries.shape
    by_head = [rows_of.transpose(1, 0, 2) for rows_of in (queries, *key_slabs, *value_slabs)]
    keep = jnp.repeat(keep_tiles.astype(jnp.float32), TILE, axis=1)
    block = pl.BlockSpec((1, rows, depth), lambda head: (head, 0, 0))
    return pl.pallas_call(
        functools.partial(attend_kernel, len(key_slabs) // 2, 1.0 / math.sqrt(depth)),
        grid=(head_count,),
        out_shape=jax.ShapeDtypeStruct((rows, head_count * depth), jnp.bfloat16),
        in_specs=[pl.BlockSpec(keep.shape, lambda head: (0, 0))] + [block] * len(by_head),
        out_specs=pl.BlockSpec((rows, depth), lambda head: (0, head)),
        compiler_params=pltpu.CompilerParams(vmem_limit_bytes=16 * 2**20),
        cost_estimate=pl.CostEstimate(flops=2 * 10**10, bytes_accessed=10**7, transcendentals=0),
        name="attend",
    )(keep, *by_head)


def halo(key_rows, value_rows):
    reach_slabs = min(2, (lax.axis_size("tm") - 1) // 2)
    lower_list = []
    upper_list = []
    for distance in range(1, reach_slabs + 1):
        lower_list.append([passed_along(rows, "tm", distance) for rows in (key_rows, value_rows)])
        upper_list.append([passed_along(rows, "tm", -distance) for rows in (key_rows, value_rows)])
    return lower_list[::-1], upper_list


def diagonal(array):
    pairs = [(4 * g + h, 4 * (g ^ 1) + (h ^ 2)) for g in range(2) for h in range(4)]
    return lax.ppermute(array, ("groups", "head"), pairs)


def all_slabs(lower, own, upper):
    ordered = lower + [own] + upper
    return [[slab[which] for slab in ordered] for which in (0, 1)]


def any_mesh(queries, key_rows, value_rows, keep_tiles, out_weight, gate_scale):
    lower, upper = halo(key_rows, value_rows)
    key_slabs, value_slabs = all_slabs(lower, (key_rows, value_rows), upper)
    attended = attend(queries, key_slabs, value_slabs, keep_tiles)
    partial_value = jnp.dot(
        attended,
        lax.all_gather(out_weight, "tm", axis=1, tiled=True),
        preferred_element_type=jnp.float32,
    )
    summed = lax.psum_scatter(
        partial_value.astype(jnp.bfloat16), "head", scatter_dimension=1, tiled=True
    ).astype(jnp.float32)
    return (gate_scale[None, :] * summed).astype(jnp.bfloat16)


def after(array, *others):
    return lax.optimization_barrier((array, *others))[0]


def f32(array):
    return array.astype(jnp.float32)


SMEM = pl.BlockSpec(memory_space=pltpu.SMEM)
WHOLE = pl.BlockSpec(memory_space=pltpu.VMEM)
LATER = pl.BlockSpec(memory_space=pl.ANY)


def local_call(kernel, outs, flags, arrays, earlier, name, flops=0, left=(), scratch=()):
    def body(*refs):
        count = len(flags) + len(arrays) + len(left)
        kernel(*refs[:count], *refs[count + len(earlier) :])

    moved = sum(array.size * array.dtype.itemsize for array in (*arrays, *left, *outs))
    return pl.pallas_call(
        body,
        out_shape=outs,
        in_specs=[SMEM] * len(flags)
        + [WHOLE] * len(arrays)
        + [LATER] * (len(left) + len(earlier)),
        out_specs=[WHOLE] * len(outs),
        scratch_shapes=scratch,
        compiler_params=pltpu.CompilerParams(vmem_limit_bytes=16 * 2**20),
        cost_estimate=pl.CostEstimate(flops=flops, bytes_accessed=moved, transcendentals=0),
        name=name,
    )(*[jnp.int32(flag).reshape(1) for flag in flags], *arrays, *left, *earlier)


def terms(rows_of, blocks, role, first, cost, earlier=()):
    rows, depth = rows_of[0][0].shape
    width = blocks[0].shape[2]
    flat = [array for core in rows_of for array in core]

    def kernel(role_ref, first_ref, *refs):
        rows_refs, block_refs = refs[:4], refs[4:8]
        near_ref, far_ref, near_given_ref, far_given_ref, held_rows, weight, landed = refs[8:]
        out_refs = ((near_ref, far_ref), (near_given_ref, far_given_ref))

        def weight_copies(slot, index):
            return [
                pltpu.make_async_copy(
                    block_refs[index].at[core],
                    weight.at[slot, pl.ds(core * depth, depth)],
                    landed.at[4 + 2 * slot + core],
                )
                for core in (0, 1)
            ]

        def start_weights(odd, second):
            for slot in (1, 0):
                for copy in weight_copies(slot, odd + 2 * (slot ^ second)):
                    copy.start()

        for odd in (0, 1):
            for second in (0, 1):
                chosen = (role_ref[0] == odd) & (first_ref[0] == 1 - second)
                pl.when(chosen)(functools.partial(start_weights, odd, second))
        rows_copies = [
            pltpu.make_async_copy(
                rows_ref,
                held_rows.at[pl.ds(index % 2 * rows, rows), pl.ds(index // 2 * depth, depth)],
                landed.at[index],
            )
            for index, rows_ref in enumerate(rows_refs)
        ]
        for copy in rows_copies:
            copy.start()
        for copy in rows_copies:
            copy.wait()
        for slot in (1, 0):
            for copy in weight_copies(slot, 0):
                copy.wait()
            total = jnp.dot(held_rows[...], weight[slot], preferred_element_type=jnp.float32)
            for video, out_ref in enumerate(out_refs[slot]):
                out_ref[...] = total[video * rows : (video + 1) * rows].astype(out_ref.dtype)

    kinds = (jnp.float32, jnp.bfloat16, jnp.bfloat16, jnp.bfloat16)
    outs = [jax.ShapeDtypeStruct((rows, width), kind) for kind in kinds]
    scratch = [
        pltpu.VMEM((2 * rows, 2 * depth), jnp.bfloat16),
        pltpu.VMEM((2, 2 * depth, width), jnp.bfloat16),
        pltpu.SemaphoreType.DMA((8,)),
    ]
    left = (*flat, *blocks)
    return local_call(
        kernel, outs, (role, first), (), earlier, "terms", cost, left=left, scratch=scratch
    )


def held(arrays, earlier, cost=0):
    return pl.pallas_call(
        lambda *refs: None,
        out_shape=[jax.ShapeDtypeStruct(array.shape, array.dtype) for array in arrays],
        in_specs=[LATER] * (len(arrays) + len(earlier)),
        out_specs=[LATER] * len(arrays),
        input_output_aliases={index: index for index in range(len(arrays))},
        cost_estimate=pl.CostEstimate(flops=cost, bytes_accessed=0, transcendentals=0),
        name="held",
    )(*arrays, *earlier)


def gated(gate_scale, parts, video, earlier=()):
    rows = parts[0][0][0].shape[0]
    width = sum(near[0].shape[1] for near, _ in parts)

    def kernel(video_ref, gate_ref, *refs):
        part_refs, out_ref = list(refs[:-1]), refs[-1]
        starts = video_ref[0] * width, (1 - video_ref[0]) * width
        column = 0
        for part in parts:
            for start, half in zip(starts, part):
                total = f32(part_refs.pop(0)[...])
                for _ in half[1:]:
                    total = total + f32(part_refs.pop(0)[...])
                columns = pl.ds(pl.multiple_of(start + column, TILE), total.shape[1])
                out_ref[:, columns] = (gate_ref[:, columns] * total).astype(out_ref.dtype)
            column += part[0][0].shape[1]

    arrays = [array for part in parts for half in part for array in half]
    out = jax.ShapeDtypeStruct((rows, 2 * width), jnp.bfloat16)
    arrays = (gate_scale.reshape(1, -1), *arrays)
    return local_call(kernel, [out], (video,), arrays, earlier, "gated")[0]


def square_mesh(queries, key_rows, value_rows, keep_tiles, out_weight, gate_scale):
    video = lax.axis_index("groups")
    slab = lax.axis_index("tm")
    head = lax.axis_index("head")
    width = out_weight.shape[1] // 2
    cut = width - CUT
    role = (slab ^ head) & 1
    first = slab // 2 == head // 2

    def passed(array, slab_mask, head_mask, odd):
        pairs = [
            (4 * t + h, 4 * (t ^ slab_mask) + (h ^ head_mask))
            for t in range(4)
            for h in range(4)
            if (t ^ h) & 1 == odd
        ]
        return lax.ppermute(array, ("tm", "head"), pairs)

    lower, upper = halo(key_rows, value_rows)
    half = lax.dynamic_slice_in_dim(out_weight, video * width, width, 1)
    both = jnp.stack([half, passed(half, 0, 1, 1)])
    early, late = lax.optimization_barrier((both[..., :cut], both[..., cut:], lower[-1][0], upper[0][0]))[:2]
    block_0 = [early, late]
    block_2 = [passed(early, 2, 0, 0)]
    block_1 = [passed(early, 1, 0, 0)]

    key_slabs, value_slabs = all_slabs(lower, (key_rows, value_rows), upper)
    mine = attend(queries, key_slabs, value_slabs, keep_tiles)
    mine, block_2[0], block_1[0] = lax.optimization_barrier((mine, block_2[0], block_1[0]))
    other = swapped(mine, "groups", 1)
    rows_of = (mine, other), (swapped(mine, "head", 1), swapped(other, "head", 1))
    block_2 += held([passed(late, 2, 0, 0)], [], 100 * 2**33)
    block_1.append(passed(after(late, block_2[0]), 1, 0, 0))
    block_3 = [passed(block, 1, 0, 0) for block in block_2]
    block_3[0] = held([block_3[0]], [], 100 * 2**33)[0]
    parts = list(zip(block_0, block_1, block_2, block_3))

    cost = 100 * 2**33
    summed = []
    given = []
    for part in parts:
        near, far, near_given, far_given = terms(rows_of, part, role, first, cost, given)
        given = [near_given]
        arrived = [swapped(near_given, "head", 2), swapped(far, "groups", 1), diagonal(far_given)]
        if not summed:
            arrived = held(arrived, [], 100 * 2**33)
        summed.append(((near, arrived[0]), arrived[1:]))
    return gated(gate_scale, summed, video)


def solution(mesh):
    placed = (
        P(("groups", "tm"), "head", None),
        P(("groups", "tm"), "head", None),
        P(("groups", "tm"), "head", None),
        P(("groups", "tm"), None),
        P("head", "tm"),
        P(("groups", "head")),
    )
    sizes = (mesh.shape["groups"], mesh.shape["tm"], mesh.shape["head"])
    return jax.shard_map(
        square_mesh if sizes == (2, 4, 4) else any_mesh,
        mesh=mesh,
        in_specs=placed,
        out_specs=P(("groups", "tm"), "head"),
        check_vma=False,
    )
```

```python
import functools
import math

import jax
import jax.numpy as jnp
from jax import lax
from jax.experimental import pallas as pl
from jax.experimental.pallas import tpu as pltpu
from jax.sharding import PartitionSpec as P

TILE = 128
STARTS = 0, 2


def passed_along(array, axis, by):
    count = lax.axis_size(axis)
    return lax.ppermute(array, axis, [(i, (i + by) % count) for i in range(count)])


def swapped(array, axis, mask):
    count = lax.axis_size(axis)
    return lax.ppermute(array, axis, [(i, i ^ mask) for i in range(count)])


def attend_kernel(reach, score_scale, keep_ref, queries_ref, *refs):
    key_refs, value_refs, out_ref = refs[: 2 * reach + 1], refs[2 * reach + 1 : -1], refs[-1]
    tiles = queries_ref.shape[1] // TILE
    scale = score_scale * math.log2(math.e)
    for tile in range(tiles):
        query_tile = queries_ref[0, tile * TILE : (tile + 1) * TILE]
        scores = []
        for slab, key_ref in enumerate(key_refs):
            raw = lax.dot_general(
                query_tile, key_ref[0], (((1,), (1,)), ((), ())), preferred_element_type=jnp.float32
            )
            keep = keep_ref[tile : tile + 1, slab * tiles * TILE : (slab + 1) * tiles * TILE]
            scores.append(jnp.where(keep > 0, raw, -jnp.inf))
        peak = scores[0].max(axis=1, keepdims=True)
        for block in scores[1:]:
            peak = jnp.maximum(peak, block.max(axis=1, keepdims=True))
        total, out = 0.0, 0.0
        for block, value_ref in zip(scores, value_refs):
            weights = jnp.exp2((block - peak) * scale)
            total = total + weights.sum(axis=1, keepdims=True)
            out = out + jnp.dot(
                weights.astype(jnp.bfloat16), value_ref[0], preferred_element_type=jnp.float32
            )
        out_ref[tile * TILE : (tile + 1) * TILE] = (out / total).astype(out_ref.dtype)


def attend(queries, key_slabs, value_slabs, keep_tiles):
    rows, head_count, depth = queries.shape
    by_head = [rows_of.transpose(1, 0, 2) for rows_of in (queries, *key_slabs, *value_slabs)]
    keep = jnp.repeat(keep_tiles.astype(jnp.float32), TILE, axis=1)
    block = pl.BlockSpec((1, rows, depth), lambda head: (head, 0, 0))
    return pl.pallas_call(
        functools.partial(attend_kernel, len(key_slabs) // 2, 1.0 / math.sqrt(depth)),
        grid=(head_count,),
        out_shape=jax.ShapeDtypeStruct((rows, head_count * depth), jnp.bfloat16),
        in_specs=[pl.BlockSpec(keep.shape, lambda head: (0, 0))] + [block] * len(by_head),
        out_specs=pl.BlockSpec((rows, depth), lambda head: (0, head)),
        compiler_params=pltpu.CompilerParams(vmem_limit_bytes=16 * 2**20),
        cost_estimate=pl.CostEstimate(flops=2 * 10**10, bytes_accessed=10**7, transcendentals=0),
        name="attend",
    )(keep, *by_head)


def halo(key_rows, value_rows):
    reach_slabs = min(2, (lax.axis_size("tm") - 1) // 2)
    lower_list = []
    upper_list = []
    for distance in range(1, reach_slabs + 1):
        lower_list.append([passed_along(rows, "tm", distance) for rows in (key_rows, value_rows)])
        upper_list.append([passed_along(rows, "tm", -distance) for rows in (key_rows, value_rows)])
    return lower_list[::-1], upper_list


def diagonal(array):
    pairs = [(4 * g + h, 4 * (g ^ 1) + (h ^ 2)) for g in range(2) for h in range(4)]
    return lax.ppermute(array, ("groups", "head"), pairs)


def all_slabs(lower, own, upper):
    ordered = lower + [own] + upper
    return [[slab[which] for slab in ordered] for which in (0, 1)]


def any_mesh(queries, key_rows, value_rows, keep_tiles, out_weight, gate_scale):
    lower, upper = halo(key_rows, value_rows)
    key_slabs, value_slabs = all_slabs(lower, (key_rows, value_rows), upper)
    attended = attend(queries, key_slabs, value_slabs, keep_tiles)
    partial_value = jnp.dot(
        attended,
        lax.all_gather(out_weight, "tm", axis=1, tiled=True),
        preferred_element_type=jnp.float32,
    )
    summed = lax.psum_scatter(
        partial_value.astype(jnp.bfloat16), "head", scatter_dimension=1, tiled=True
    ).astype(jnp.float32)
    return (gate_scale[None, :] * summed).astype(jnp.bfloat16)


def after(array, *others):
    return lax.optimization_barrier((array, *others))[0]


def f32(array):
    return array.astype(jnp.float32)


SMEM = pl.BlockSpec(memory_space=pltpu.SMEM)
WHOLE = pl.BlockSpec(memory_space=pltpu.VMEM)
LATER = pl.BlockSpec(memory_space=pl.ANY)


def local_call(kernel, outs, flags, arrays, earlier, name, flops=0, left=(), scratch=()):
    def body(*refs):
        count = len(flags) + len(arrays) + len(left)
        kernel(*refs[:count], *refs[count + len(earlier) :])

    moved = sum(array.size * array.dtype.itemsize for array in (*arrays, *left, *outs))
    return pl.pallas_call(
        body,
        out_shape=outs,
        in_specs=[SMEM] * len(flags)
        + [WHOLE] * len(arrays)
        + [LATER] * (len(left) + len(earlier)),
        out_specs=[WHOLE] * len(outs),
        scratch_shapes=scratch,
        compiler_params=pltpu.CompilerParams(vmem_limit_bytes=16 * 2**20),
        cost_estimate=pl.CostEstimate(flops=flops, bytes_accessed=moved, transcendentals=0),
        name=name,
    )(*[jnp.int32(flag).reshape(1) for flag in flags], *arrays, *left, *earlier)


def terms(rows_of, blocks, role, first, cost, earlier=()):
    rows, depth = rows_of[0][0].shape
    width = blocks[0][0].shape[2]
    starts = [column for _, column in blocks]
    blocks = [block for block, _ in blocks]
    flat = [array for core in rows_of for array in core]

    def kernel(role_ref, first_ref, *refs):
        rows_refs, block_refs = refs[:4], refs[4:8]
        near_ref, far_ref, near_given_ref, far_given_ref, held_rows, weight, landed = refs[8:]
        out_refs = ((near_ref, far_ref), (near_given_ref, far_given_ref))

        def weight_copies(slot, index):
            return [
                pltpu.make_async_copy(
                    block_refs[index].at[core, :, pl.ds(starts[index], width)],
                    weight.at[slot, pl.ds(core * depth, depth)],
                    landed.at[4 + 2 * slot + core],
                )
                for core in (0, 1)
            ]

        def start_weights(odd, second):
            for slot in (1, 0):
                for copy in weight_copies(slot, odd + 2 * (slot ^ second)):
                    copy.start()

        for odd in (0, 1):
            for second in (0, 1):
                chosen = (role_ref[0] == odd) & (first_ref[0] == 1 - second)
                pl.when(chosen)(functools.partial(start_weights, odd, second))
        rows_copies = [
            pltpu.make_async_copy(
                rows_ref,
                held_rows.at[pl.ds(index % 2 * rows, rows), pl.ds(index // 2 * depth, depth)],
                landed.at[index],
            )
            for index, rows_ref in enumerate(rows_refs)
        ]
        for copy in rows_copies:
            copy.start()
        for copy in rows_copies:
            copy.wait()
        for slot in (1, 0):
            for copy in weight_copies(slot, 0):
                copy.wait()
            total = jnp.dot(held_rows[...], weight[slot], preferred_element_type=jnp.float32)
            for video, out_ref in enumerate(out_refs[slot]):
                out_ref[...] = total[video * rows : (video + 1) * rows].astype(out_ref.dtype)

    kinds = (jnp.float32, jnp.bfloat16, jnp.bfloat16, jnp.bfloat16)
    outs = [jax.ShapeDtypeStruct((rows, width), kind) for kind in kinds]
    scratch = [
        pltpu.VMEM((2 * rows, 2 * depth), jnp.bfloat16),
        pltpu.VMEM((2, 2 * depth, width), jnp.bfloat16),
        pltpu.SemaphoreType.DMA((8,)),
    ]
    left = (*flat, *blocks)
    return local_call(
        kernel, outs, (role, first), (), earlier, "terms", cost, left=left, scratch=scratch
    )


def held(arrays, earlier, cost=0):
    return pl.pallas_call(
        lambda *refs: None,
        out_shape=[jax.ShapeDtypeStruct(array.shape, array.dtype) for array in arrays],
        in_specs=[LATER] * (len(arrays) + len(earlier)),
        out_specs=[LATER] * len(arrays),
        input_output_aliases={index: index for index in range(len(arrays))},
        cost_estimate=pl.CostEstimate(flops=cost, bytes_accessed=0, transcendentals=0),
        name="held",
    )(*arrays, *earlier)


def gated(gate_scale, parts, video, earlier=()):
    rows = parts[0][0][0].shape[0]
    width = sum(near[0].shape[1] for near, _ in parts)

    def kernel(video_ref, gate_ref, *refs):
        part_refs, out_ref = list(refs[:-1]), refs[-1]
        starts = video_ref[0] * width, (1 - video_ref[0]) * width
        column = 0
        for part in parts:
            for start, half in zip(starts, part):
                total = f32(part_refs.pop(0)[...])
                for _ in half[1:]:
                    total = total + f32(part_refs.pop(0)[...])
                columns = pl.ds(pl.multiple_of(start + column, TILE), total.shape[1])
                out_ref[:, columns] = (gate_ref[:, columns] * total).astype(out_ref.dtype)
            column += part[0][0].shape[1]

    arrays = [array for part in parts for half in part for array in half]
    out = jax.ShapeDtypeStruct((rows, 2 * width), jnp.bfloat16)
    arrays = (gate_scale.reshape(1, -1), *arrays)
    return local_call(kernel, [out], (video,), arrays, earlier, "gated")[0]


def square_mesh(queries, key_rows, value_rows, keep_tiles, out_weight, gate_scale):
    video = lax.axis_index("groups")
    slab = lax.axis_index("tm")
    head = lax.axis_index("head")
    width = out_weight.shape[1] // 2
    starts = [width * place // 5 // TILE * TILE for place in STARTS]
    spans = list(zip(starts, starts[1:] + [width]))
    role = (slab ^ head) & 1
    first = slab // 2 == head // 2

    def passed(array, slab_mask, head_mask, odd):
        pairs = [
            (4 * t + h, 4 * (t ^ slab_mask) + (h ^ head_mask))
            for t in range(4)
            for h in range(4)
            if (t ^ h) & 1 == odd
        ]
        return lax.ppermute(array, ("tm", "head"), pairs)

    lower, upper = halo(key_rows, value_rows)
    half = lax.dynamic_slice_in_dim(out_weight, video * width, width, 1)
    both = jnp.stack([half, passed(half, 0, 1, 1)])
    both, *block_0 = lax.optimization_barrier(
        (both, *[both[..., start:end] for start, end in spans], lower[-1][0], upper[0][0])
    )[: len(spans) + 1]
    block_2 = [passed(part, 2, 0, 0) for part in block_0]
    block_1 = passed(both, 1, 0, 0)

    key_slabs, value_slabs = all_slabs(lower, (key_rows, value_rows), upper)
    mine = attend(queries, key_slabs, value_slabs, keep_tiles)
    to_core = mine
    block_2[0], block_1 = lax.optimization_barrier((block_2[0], block_1))
    other = swapped(mine, "groups", 1)
    rows_of = (mine, other), (swapped(to_core, "head", 1), swapped(other, "head", 1))
    block_2[1:] = [held([block], [], 100 * 2**33)[0] for block in block_2[1:]]
    block_3 = [passed(block, 1, 0, 0) for block in block_2]
    block_3[0] = held([block_3[0]], [], 100 * 2**33)[0]
    parts = [
        [(block_0[i], 0), (block_1, spans[i][0]), (block_2[i], 0), (block_3[i], 0)]
        for i in range(len(spans))
    ]

    cost = 100 * 2**33
    summed = []
    given = []
    for part in parts:
        near, far, near_given, far_given = terms(rows_of, part, role, first, cost, given)
        given = [near_given]
        arrived = [swapped(near_given, "head", 2), swapped(far, "groups", 1), diagonal(far_given)]
        if len(summed) < len(parts) - 1:
            arrived = held(arrived, [], 100 * 2**33)
        summed.append(((near, arrived[0]), arrived[1:]))
    return gated(gate_scale, summed, video)


def solution(mesh):
    placed = (
        P(("groups", "tm"), "head", None),
        P(("groups", "tm"), "head", None),
        P(("groups", "tm"), "head", None),
        P(("groups", "tm"), None),
        P("head", "tm"),
        P(("groups", "head")),
    )
    sizes = (mesh.shape["groups"], mesh.shape["tm"], mesh.shape["head"])
    return jax.shard_map(
        square_mesh if sizes == (2, 4, 4) else any_mesh,
        mesh=mesh,
        in_specs=placed,
        out_specs=P(("groups", "tm"), "head"),
        check_vma=False,
    )
```

```python
import functools
import math

import jax
import jax.numpy as jnp
from jax import lax
from jax.experimental import pallas as pl
from jax.experimental.pallas import tpu as pltpu
from jax.sharding import PartitionSpec as P

TILE = 128
STARTS = 0, 2


def passed_along(array, axis, by):
    count = lax.axis_size(axis)
    return lax.ppermute(array, axis, [(i, (i + by) % count) for i in range(count)])


def swapped(array, axis, mask):
    count = lax.axis_size(axis)
    return lax.ppermute(array, axis, [(i, i ^ mask) for i in range(count)])


def attend_kernel(reach, score_scale, keep_ref, queries_ref, *refs):
    key_refs, value_refs, out_ref = refs[: 2 * reach + 1], refs[2 * reach + 1 : -1], refs[-1]
    tiles = queries_ref.shape[1] // TILE
    scale = score_scale * math.log2(math.e)
    for tile in range(tiles):
        query_tile = queries_ref[0, tile * TILE : (tile + 1) * TILE]
        scores = []
        for slab, key_ref in enumerate(key_refs):
            raw = lax.dot_general(
                query_tile, key_ref[0], (((1,), (1,)), ((), ())), preferred_element_type=jnp.float32
            )
            keep = keep_ref[tile : tile + 1, slab * tiles * TILE : (slab + 1) * tiles * TILE]
            scores.append(jnp.where(keep > 0, raw, -jnp.inf))
        peak = scores[0].max(axis=1, keepdims=True)
        for block in scores[1:]:
            peak = jnp.maximum(peak, block.max(axis=1, keepdims=True))
        total, out = 0.0, 0.0
        for block, value_ref in zip(scores, value_refs):
            weights = jnp.exp2((block - peak) * scale)
            total = total + weights.sum(axis=1, keepdims=True)
            out = out + jnp.dot(
                weights.astype(jnp.bfloat16), value_ref[0], preferred_element_type=jnp.float32
            )
        out_ref[tile * TILE : (tile + 1) * TILE] = (out / total).astype(out_ref.dtype)


def attend(queries, key_slabs, value_slabs, keep_tiles):
    rows, head_count, depth = queries.shape
    by_head = [rows_of.transpose(1, 0, 2) for rows_of in (queries, *key_slabs, *value_slabs)]
    keep = jnp.repeat(keep_tiles.astype(jnp.float32), TILE, axis=1)
    block = pl.BlockSpec((1, rows, depth), lambda head: (head, 0, 0))
    return pl.pallas_call(
        functools.partial(attend_kernel, len(key_slabs) // 2, 1.0 / math.sqrt(depth)),
        grid=(head_count,),
        out_shape=jax.ShapeDtypeStruct((rows, head_count * depth), jnp.bfloat16),
        in_specs=[pl.BlockSpec(keep.shape, lambda head: (0, 0))] + [block] * len(by_head),
        out_specs=pl.BlockSpec((rows, depth), lambda head: (0, head)),
        compiler_params=pltpu.CompilerParams(vmem_limit_bytes=16 * 2**20),
        cost_estimate=pl.CostEstimate(flops=2 * 10**10, bytes_accessed=10**7, transcendentals=0),
        name="attend",
    )(keep, *by_head)


def halo(key_rows, value_rows):
    reach_slabs = min(2, (lax.axis_size("tm") - 1) // 2)
    lower_list = []
    upper_list = []
    for distance in range(1, reach_slabs + 1):
        lower_list.append([passed_along(rows, "tm", distance) for rows in (key_rows, value_rows)])
        upper_list.append([passed_along(rows, "tm", -distance) for rows in (key_rows, value_rows)])
    return lower_list[::-1], upper_list


def diagonal(array):
    pairs = [(4 * g + h, 4 * (g ^ 1) + (h ^ 2)) for g in range(2) for h in range(4)]
    return lax.ppermute(array, ("groups", "head"), pairs)


def all_slabs(lower, own, upper):
    ordered = lower + [own] + upper
    return [[slab[which] for slab in ordered] for which in (0, 1)]


def any_mesh(queries, key_rows, value_rows, keep_tiles, out_weight, gate_scale):
    lower, upper = halo(key_rows, value_rows)
    key_slabs, value_slabs = all_slabs(lower, (key_rows, value_rows), upper)
    attended = attend(queries, key_slabs, value_slabs, keep_tiles)
    partial_value = jnp.dot(
        attended,
        lax.all_gather(out_weight, "tm", axis=1, tiled=True),
        preferred_element_type=jnp.float32,
    )
    summed = lax.psum_scatter(
        partial_value.astype(jnp.bfloat16), "head", scatter_dimension=1, tiled=True
    ).astype(jnp.float32)
    return (gate_scale[None, :] * summed).astype(jnp.bfloat16)


def after(array, *others):
    return lax.optimization_barrier((array, *others))[0]


def f32(array):
    return array.astype(jnp.float32)


SMEM = pl.BlockSpec(memory_space=pltpu.SMEM)
WHOLE = pl.BlockSpec(memory_space=pltpu.VMEM)
LATER = pl.BlockSpec(memory_space=pl.ANY)


def local_call(kernel, outs, flags, arrays, earlier, name, flops=0, left=(), scratch=()):
    def body(*refs):
        count = len(flags) + len(arrays) + len(left)
        kernel(*refs[:count], *refs[count + len(earlier) :])

    moved = sum(array.size * array.dtype.itemsize for array in (*arrays, *left, *outs))
    return pl.pallas_call(
        body,
        out_shape=outs,
        in_specs=[SMEM] * len(flags)
        + [WHOLE] * len(arrays)
        + [LATER] * (len(left) + len(earlier)),
        out_specs=[WHOLE] * len(outs),
        scratch_shapes=scratch,
        compiler_params=pltpu.CompilerParams(vmem_limit_bytes=16 * 2**20),
        cost_estimate=pl.CostEstimate(flops=flops, bytes_accessed=moved, transcendentals=0),
        name=name,
    )(*[jnp.int32(flag).reshape(1) for flag in flags], *arrays, *left, *earlier)


def terms(rows_of, blocks, role, first, cost, earlier=()):
    rows, depth = rows_of[0][0].shape
    width = blocks[0][0].shape[2]
    starts = [column for _, column in blocks]
    blocks = [block for block, _ in blocks]
    flat = [array for core in rows_of for array in core]

    def kernel(role_ref, first_ref, *refs):
        rows_refs, block_refs = refs[:4], refs[4:8]
        near_ref, far_ref, near_given_ref, far_given_ref, held_rows, weight, landed = refs[8:]
        out_refs = ((near_ref, far_ref), (near_given_ref, far_given_ref))

        def weight_copies(slot, index):
            return [
                pltpu.make_async_copy(
                    block_refs[index].at[core, :, pl.ds(starts[index], width)],
                    weight.at[slot, pl.ds(core * depth, depth)],
                    landed.at[4 + 2 * slot + core],
                )
                for core in (0, 1)
            ]

        def start_weights(odd, second):
            for slot in (1, 0):
                for copy in weight_copies(slot, odd + 2 * (slot ^ second)):
                    copy.start()

        for odd in (0, 1):
            for second in (0, 1):
                chosen = (role_ref[0] == odd) & (first_ref[0] == 1 - second)
                pl.when(chosen)(functools.partial(start_weights, odd, second))
        rows_copies = [
            pltpu.make_async_copy(
                rows_ref,
                held_rows.at[pl.ds(index % 2 * rows, rows), pl.ds(index // 2 * depth, depth)],
                landed.at[index],
            )
            for index, rows_ref in enumerate(rows_refs)
        ]
        for copy in rows_copies:
            copy.start()
        for copy in rows_copies:
            copy.wait()
        for slot in (1, 0):
            for copy in weight_copies(slot, 0):
                copy.wait()
            total = jnp.dot(held_rows[...], weight[slot], preferred_element_type=jnp.float32)
            for video, out_ref in enumerate(out_refs[slot]):
                out_ref[...] = total[video * rows : (video + 1) * rows].astype(out_ref.dtype)

    kinds = (jnp.float32, jnp.bfloat16, jnp.bfloat16, jnp.bfloat16)
    outs = [jax.ShapeDtypeStruct((rows, width), kind) for kind in kinds]
    scratch = [
        pltpu.VMEM((2 * rows, 2 * depth), jnp.bfloat16),
        pltpu.VMEM((2, 2 * depth, width), jnp.bfloat16),
        pltpu.SemaphoreType.DMA((8,)),
    ]
    left = (*flat, *blocks)
    return local_call(
        kernel, outs, (role, first), (), earlier, "terms", cost, left=left, scratch=scratch
    )


def early_terms(rows_of, blocks, role, cost):
    rows, depth = rows_of[0][0].shape
    width = blocks[0][0].shape[2]
    starts = [column for _, column in blocks]
    flat = [array for core in rows_of for array in core]

    def kernel(role_ref, *refs):
        rows_refs, block_refs, out_ref = refs[:4], refs[4:6], refs[6]
        held_rows, weight, landed = refs[7:]
        copies = row_copies(rows_refs, held_rows, landed)
        for odd in (0, 1):
            for copy in weight_copies(block_refs[odd], starts[odd], weight, landed):
                pl.when(role_ref[0] == odd)(copy.start)
        for copy in copies:
            copy.start()
        for copy in copies + weight_copies(block_refs[0], starts[0], weight, landed):
            copy.wait()
        total = jnp.dot(held_rows[...], weight[...], preferred_element_type=jnp.float32)
        for video in (0, 1):
            out_ref[video] = total[video * rows : (video + 1) * rows]

    out = jax.ShapeDtypeStruct((2, rows, width), jnp.float32)
    left = (*flat, *[block for block, _ in blocks])
    scratch = term_scratch(rows, depth, width)
    return local_call(
        kernel, [out], (role,), (), (), "early_terms", cost, left=left, scratch=scratch
    )[0]


def late_terms(rows_of, blocks, role, first, early, cost, earlier=()):
    rows, depth = rows_of[0][0].shape
    width = blocks[0][0].shape[2]
    starts = [column for _, column in blocks]
    flat = [array for core in rows_of for array in core]

    def kernel(role_ref, first_ref, early_ref, *refs):
        rows_refs, block_refs = refs[:4], refs[4:6]
        near_ref, far_ref, near_given_ref, far_given_ref, held_rows, weight, landed = refs[6:]
        copies = row_copies(rows_refs, held_rows, landed)
        for odd in (0, 1):
            for copy in weight_copies(block_refs[odd], starts[odd], weight, landed):
                pl.when(role_ref[0] == odd)(copy.start)
        for copy in copies:
            copy.start()
        for copy in copies + weight_copies(block_refs[0], starts[0], weight, landed):
            copy.wait()
        total = jnp.dot(held_rows[...], weight[...], preferred_element_type=jnp.float32)
        kept_refs, given_refs = (near_ref, far_ref), (near_given_ref, far_given_ref)
        for stays, late_refs, early_refs in (
            (1, given_refs, kept_refs),
            (0, kept_refs, given_refs),
        ):

            @pl.when(first_ref[0] == stays)
            def _():
                for video in (0, 1):
                    late = total[video * rows : (video + 1) * rows]
                    late_refs[video][...] = late.astype(late_refs[video].dtype)
                    early_refs[video][...] = early_ref[video].astype(early_refs[video].dtype)

    kinds = (jnp.float32, jnp.bfloat16, jnp.bfloat16, jnp.bfloat16)
    outs = [jax.ShapeDtypeStruct((rows, width), kind) for kind in kinds]
    left = (*flat, *[block for block, _ in blocks])
    scratch = term_scratch(rows, depth, width)
    return local_call(
        kernel, outs, (role, first), (early,), earlier, "late_terms", cost, left=left, scratch=scratch
    )


def row_copies(rows_refs, held_rows, landed):
    rows, depth = rows_refs[0].shape
    return [
        pltpu.make_async_copy(
            rows_ref,
            held_rows.at[pl.ds(index % 2 * rows, rows), pl.ds(index // 2 * depth, depth)],
            landed.at[index],
        )
        for index, rows_ref in enumerate(rows_refs)
    ]


def weight_copies(block_ref, start, weight, landed):
    depth, width = weight.shape[0] // 2, weight.shape[1]
    return [
        pltpu.make_async_copy(
            block_ref.at[core, :, pl.ds(start, width)],
            weight.at[pl.ds(core * depth, depth)],
            landed.at[4 + core],
        )
        for core in (0, 1)
    ]


def term_scratch(rows, depth, width):
    return [
        pltpu.VMEM((2 * rows, 2 * depth), jnp.bfloat16),
        pltpu.VMEM((2 * depth, width), jnp.bfloat16),
        pltpu.SemaphoreType.DMA((6,)),
    ]


def held(arrays, earlier, cost=0):
    return pl.pallas_call(
        lambda *refs: None,
        out_shape=[jax.ShapeDtypeStruct(array.shape, array.dtype) for array in arrays],
        in_specs=[LATER] * (len(arrays) + len(earlier)),
        out_specs=[LATER] * len(arrays),
        input_output_aliases={index: index for index in range(len(arrays))},
        cost_estimate=pl.CostEstimate(flops=cost, bytes_accessed=0, transcendentals=0),
        name="held",
    )(*arrays, *earlier)


def gated(gate_scale, parts, video, earlier=()):
    rows = parts[0][0][0].shape[0]
    width = sum(near[0].shape[1] for near, _ in parts)

    def kernel(video_ref, gate_ref, *refs):
        part_refs, out_ref = list(refs[:-1]), refs[-1]
        starts = video_ref[0] * width, (1 - video_ref[0]) * width
        column = 0
        for part in parts:
            for start, half in zip(starts, part):
                total = f32(part_refs.pop(0)[...])
                for _ in half[1:]:
                    total = total + f32(part_refs.pop(0)[...])
                columns = pl.ds(pl.multiple_of(start + column, TILE), total.shape[1])
                out_ref[:, columns] = (gate_ref[:, columns] * total).astype(out_ref.dtype)
            column += part[0][0].shape[1]

    arrays = [array for part in parts for half in part for array in half]
    out = jax.ShapeDtypeStruct((rows, 2 * width), jnp.bfloat16)
    arrays = (gate_scale.reshape(1, -1), *arrays)
    return local_call(kernel, [out], (video,), arrays, earlier, "gated")[0]


def square_mesh(queries, key_rows, value_rows, keep_tiles, out_weight, gate_scale):
    video = lax.axis_index("groups")
    slab = lax.axis_index("tm")
    head = lax.axis_index("head")
    width = out_weight.shape[1] // 2
    starts = [width * place // 5 // TILE * TILE for place in STARTS]
    spans = list(zip(starts, starts[1:] + [width]))
    role = (slab ^ head) & 1
    first = slab // 2 == head // 2

    def passed(array, slab_mask, head_mask, odd):
        pairs = [
            (4 * t + h, 4 * (t ^ slab_mask) + (h ^ head_mask))
            for t in range(4)
            for h in range(4)
            if (t ^ h) & 1 == odd
        ]
        return lax.ppermute(array, ("tm", "head"), pairs)

    lower, upper = halo(key_rows, value_rows)
    half = lax.dynamic_slice_in_dim(out_weight, video * width, width, 1)
    both = jnp.stack([half, passed(half, 0, 1, 1)])
    both, *block_0 = lax.optimization_barrier(
        (both, *[both[..., start:end] for start, end in spans], lower[-1][0], upper[0][0])
    )[: len(spans) + 1]
    block_2 = [passed(part, 2, 0, 0) for part in block_0]
    block_1 = passed(both, 1, 0, 0)

    key_slabs, value_slabs = all_slabs(lower, (key_rows, value_rows), upper)
    mine = attend(queries, key_slabs, value_slabs, keep_tiles)
    to_core, block_1 = lax.optimization_barrier((mine, block_1))
    other = swapped(mine, "groups", 1)
    mine_core = held([swapped(to_core, "head", 1)], [], 100 * 2**33)[0]
    rows_of = (mine, other), (mine_core, swapped(after(other, mine_core), "head", 1))
    block_2[1:] = [held([block], [], 100 * 2**33)[0] for block in block_2[1:]]
    block_3 = [passed(block, 1, 0, 0) for block in block_2]
    block_3[0] = held([block_3[0]], [], 100 * 2**33)[0]
    parts = [
        [(block_0[i], 0), (block_1, spans[i][0]), (block_2[i], 0), (block_3[i], 0)]
        for i in range(len(spans))
    ]

    cost = 100 * 2**33
    summed = []
    early = early_terms(rows_of, parts[-1][:2], role, 0)
    given = [early]
    for part in parts:
        if len(summed) < len(parts) - 1:
            near, far, near_given, far_given = terms(rows_of, part, role, first, cost, given)
            given = [near_given]
        else:
            near, far, near_given, far_given = late_terms(
                rows_of, part[2:], role, first, early, cost, given
            )
        arrived = [swapped(near_given, "head", 2), swapped(far, "groups", 1), diagonal(far_given)]
        if len(summed) < len(parts) - 1:
            arrived = held(arrived, [], 100 * 2**33)
        summed.append(((near, arrived[0]), arrived[1:]))
    return gated(gate_scale, summed, video)


def solution(mesh):
    placed = (
        P(("groups", "tm"), "head", None),
        P(("groups", "tm"), "head", None),
        P(("groups", "tm"), "head", None),
        P(("groups", "tm"), None),
        P("head", "tm"),
        P(("groups", "head")),
    )
    sizes = (mesh.shape["groups"], mesh.shape["tm"], mesh.shape["head"])
    return jax.shard_map(
        square_mesh if sizes == (2, 4, 4) else any_mesh,
        mesh=mesh,
        in_specs=placed,
        out_specs=P(("groups", "tm"), "head"),
        check_vma=False,
    )
```

```python
import functools
import math

import jax
import jax.numpy as jnp
from jax import lax
from jax.experimental import pallas as pl
from jax.experimental.pallas import tpu as pltpu
from jax.sharding import PartitionSpec as P

TILE = 128
STARTS = 0, 2


def passed_along(array, axis, by):
    count = lax.axis_size(axis)
    return lax.ppermute(array, axis, [(i, (i + by) % count) for i in range(count)])


def swapped(array, axis, mask):
    count = lax.axis_size(axis)
    return lax.ppermute(array, axis, [(i, i ^ mask) for i in range(count)])


def attend_kernel(reach, score_scale, keep_ref, queries_ref, *refs):
    key_refs, value_refs, out_ref = refs[: 2 * reach + 1], refs[2 * reach + 1 : -1], refs[-1]
    tiles = queries_ref.shape[1] // TILE
    scale = score_scale * math.log2(math.e)
    for tile in range(tiles):
        query_tile = queries_ref[0, tile * TILE : (tile + 1) * TILE]
        scores = []
        for slab, key_ref in enumerate(key_refs):
            raw = lax.dot_general(
                query_tile, key_ref[0], (((1,), (1,)), ((), ())), preferred_element_type=jnp.float32
            )
            keep = keep_ref[tile : tile + 1, slab * tiles * TILE : (slab + 1) * tiles * TILE]
            scores.append(jnp.where(keep > 0, raw, -jnp.inf))
        peak = scores[0].max(axis=1, keepdims=True)
        for block in scores[1:]:
            peak = jnp.maximum(peak, block.max(axis=1, keepdims=True))
        total, out = 0.0, 0.0
        for block, value_ref in zip(scores, value_refs):
            weights = jnp.exp2((block - peak) * scale)
            total = total + weights.sum(axis=1, keepdims=True)
            out = out + jnp.dot(
                weights.astype(jnp.bfloat16), value_ref[0], preferred_element_type=jnp.float32
            )
        out_ref[tile * TILE : (tile + 1) * TILE] = (out / total).astype(out_ref.dtype)


def attend(queries, key_slabs, value_slabs, keep_tiles):
    rows, head_count, depth = queries.shape
    by_head = [rows_of.transpose(1, 0, 2) for rows_of in (queries, *key_slabs, *value_slabs)]
    keep = jnp.repeat(keep_tiles.astype(jnp.float32), TILE, axis=1)
    block = pl.BlockSpec((1, rows, depth), lambda head: (head, 0, 0))
    return pl.pallas_call(
        functools.partial(attend_kernel, len(key_slabs) // 2, 1.0 / math.sqrt(depth)),
        grid=(head_count,),
        out_shape=jax.ShapeDtypeStruct((rows, head_count * depth), jnp.bfloat16),
        in_specs=[pl.BlockSpec(keep.shape, lambda head: (0, 0))] + [block] * len(by_head),
        out_specs=pl.BlockSpec((rows, depth), lambda head: (0, head)),
        compiler_params=pltpu.CompilerParams(vmem_limit_bytes=16 * 2**20),
        cost_estimate=pl.CostEstimate(flops=2 * 10**10, bytes_accessed=10**7, transcendentals=0),
        name="attend",
    )(keep, *by_head)


def halo(key_rows, value_rows):
    reach_slabs = min(2, (lax.axis_size("tm") - 1) // 2)
    lower_list = []
    upper_list = []
    for distance in range(1, reach_slabs + 1):
        lower_list.append([passed_along(rows, "tm", distance) for rows in (key_rows, value_rows)])
        upper_list.append([passed_along(rows, "tm", -distance) for rows in (key_rows, value_rows)])
    return lower_list[::-1], upper_list


def diagonal(array):
    pairs = [(4 * g + h, 4 * (g ^ 1) + (h ^ 2)) for g in range(2) for h in range(4)]
    return lax.ppermute(array, ("groups", "head"), pairs)


def all_slabs(lower, own, upper):
    ordered = lower + [own] + upper
    return [[slab[which] for slab in ordered] for which in (0, 1)]


def any_mesh(queries, key_rows, value_rows, keep_tiles, out_weight, gate_scale):
    lower, upper = halo(key_rows, value_rows)
    key_slabs, value_slabs = all_slabs(lower, (key_rows, value_rows), upper)
    attended = attend(queries, key_slabs, value_slabs, keep_tiles)
    partial_value = jnp.dot(
        attended,
        lax.all_gather(out_weight, "tm", axis=1, tiled=True),
        preferred_element_type=jnp.float32,
    )
    summed = lax.psum_scatter(
        partial_value.astype(jnp.bfloat16), "head", scatter_dimension=1, tiled=True
    ).astype(jnp.float32)
    return (gate_scale[None, :] * summed).astype(jnp.bfloat16)


def after(array, *others):
    return lax.optimization_barrier((array, *others))[0]


def f32(array):
    return array.astype(jnp.float32)


SMEM = pl.BlockSpec(memory_space=pltpu.SMEM)
WHOLE = pl.BlockSpec(memory_space=pltpu.VMEM)
LATER = pl.BlockSpec(memory_space=pl.ANY)


def local_call(kernel, outs, flags, arrays, earlier, name, flops=0, left=(), scratch=()):
    def body(*refs):
        count = len(flags) + len(arrays) + len(left)
        kernel(*refs[:count], *refs[count + len(earlier) :])

    moved = sum(array.size * array.dtype.itemsize for array in (*arrays, *left, *outs))
    return pl.pallas_call(
        body,
        out_shape=outs,
        in_specs=[SMEM] * len(flags)
        + [WHOLE] * len(arrays)
        + [LATER] * (len(left) + len(earlier)),
        out_specs=[WHOLE] * len(outs),
        scratch_shapes=scratch,
        compiler_params=pltpu.CompilerParams(vmem_limit_bytes=16 * 2**20),
        cost_estimate=pl.CostEstimate(flops=flops, bytes_accessed=moved, transcendentals=0),
        name=name,
    )(*[jnp.int32(flag).reshape(1) for flag in flags], *arrays, *left, *earlier)


def terms(rows_of, blocks, role, first, cost, earlier=()):
    rows, depth = rows_of[0][0].shape
    width = blocks[0][0].shape[2]
    starts = [column for _, column in blocks]
    blocks = [block for block, _ in blocks]
    flat = [array for core in rows_of for array in core]

    def kernel(role_ref, first_ref, *refs):
        rows_refs, block_refs = refs[:4], refs[4:8]
        near_ref, far_ref, near_given_ref, far_given_ref, held_rows, weight, landed = refs[8:]
        out_refs = ((near_ref, far_ref), (near_given_ref, far_given_ref))

        def weight_copies(slot, index):
            return [
                pltpu.make_async_copy(
                    block_refs[index].at[core, :, pl.ds(starts[index], width)],
                    weight.at[slot, pl.ds(core * depth, depth)],
                    landed.at[4 + 2 * slot + core],
                )
                for core in (0, 1)
            ]

        def start_weights(odd, second):
            for slot in (1, 0):
                for copy in weight_copies(slot, odd + 2 * (slot ^ second)):
                    copy.start()

        for odd in (0, 1):
            for second in (0, 1):
                chosen = (role_ref[0] == odd) & (first_ref[0] == 1 - second)
                pl.when(chosen)(functools.partial(start_weights, odd, second))
        rows_copies = [
            pltpu.make_async_copy(
                rows_ref,
                held_rows.at[pl.ds(index % 2 * rows, rows), pl.ds(index // 2 * depth, depth)],
                landed.at[index],
            )
            for index, rows_ref in enumerate(rows_refs)
        ]
        for copy in rows_copies:
            copy.start()
        for copy in rows_copies:
            copy.wait()
        for slot in (1, 0):
            for copy in weight_copies(slot, 0):
                copy.wait()
            total = jnp.dot(held_rows[...], weight[slot], preferred_element_type=jnp.float32)
            for video, out_ref in enumerate(out_refs[slot]):
                out_ref[...] = total[video * rows : (video + 1) * rows].astype(out_ref.dtype)

    kinds = (jnp.float32, jnp.bfloat16, jnp.bfloat16, jnp.bfloat16)
    outs = [jax.ShapeDtypeStruct((rows, width), kind) for kind in kinds]
    scratch = [
        pltpu.VMEM((2 * rows, 2 * depth), jnp.bfloat16),
        pltpu.VMEM((2, 2 * depth, width), jnp.bfloat16),
        pltpu.SemaphoreType.DMA((8,)),
    ]
    left = (*flat, *blocks)
    return local_call(
        kernel, outs, (role, first), (), earlier, "terms", cost, left=left, scratch=scratch
    )


def early_terms(rows_of, blocks, role, cost):
    rows, depth = rows_of[0][0].shape
    width = blocks[0][0].shape[2]
    starts = [column for _, column in blocks]
    flat = [array for core in rows_of for array in core]

    def kernel(role_ref, *refs):
        rows_refs, block_refs, out_ref = refs[:4], refs[4:6], refs[6]
        held_rows, weight, landed = refs[7:]
        copies = row_copies(rows_refs, held_rows, landed)
        for odd in (0, 1):
            for copy in weight_copies(block_refs[odd], starts[odd], weight, landed):
                pl.when(role_ref[0] == odd)(copy.start)
        for copy in copies:
            copy.start()
        for copy in copies + weight_copies(block_refs[0], starts[0], weight, landed):
            copy.wait()
        total = jnp.dot(held_rows[...], weight[...], preferred_element_type=jnp.float32)
        for video in (0, 1):
            out_ref[video] = total[video * rows : (video + 1) * rows]

    out = jax.ShapeDtypeStruct((2, rows, width), jnp.float32)
    left = (*flat, *[block for block, _ in blocks])
    scratch = term_scratch(rows, depth, width)
    return local_call(
        kernel, [out], (role,), (), (), "early_terms", cost, left=left, scratch=scratch
    )[0]


def late_terms(rows_of, blocks, role, first, early, cost, earlier=()):
    rows, depth = rows_of[0][0].shape
    width = blocks[0][0].shape[2]
    starts = [column for _, column in blocks]
    flat = [array for core in rows_of for array in core]

    def kernel(role_ref, first_ref, early_ref, *refs):
        rows_refs, block_refs = refs[:4], refs[4:6]
        near_ref, far_ref, near_given_ref, far_given_ref, held_rows, weight, landed = refs[6:]
        copies = row_copies(rows_refs, held_rows, landed)
        for odd in (0, 1):
            for copy in weight_copies(block_refs[odd], starts[odd], weight, landed):
                pl.when(role_ref[0] == odd)(copy.start)
        for copy in copies:
            copy.start()
        for copy in copies + weight_copies(block_refs[0], starts[0], weight, landed):
            copy.wait()
        total = jnp.dot(held_rows[...], weight[...], preferred_element_type=jnp.float32)
        kept_refs, given_refs = (near_ref, far_ref), (near_given_ref, far_given_ref)
        for stays, late_refs, early_refs in (
            (1, given_refs, kept_refs),
            (0, kept_refs, given_refs),
        ):

            @pl.when(first_ref[0] == stays)
            def _():
                for video in (0, 1):
                    late = total[video * rows : (video + 1) * rows]
                    late_refs[video][...] = late.astype(late_refs[video].dtype)
                    early_refs[video][...] = early_ref[video].astype(early_refs[video].dtype)

    kinds = (jnp.float32, jnp.bfloat16, jnp.bfloat16, jnp.bfloat16)
    outs = [jax.ShapeDtypeStruct((rows, width), kind) for kind in kinds]
    left = (*flat, *[block for block, _ in blocks])
    scratch = term_scratch(rows, depth, width)
    return local_call(
        kernel, outs, (role, first), (early,), earlier, "late_terms", cost, left=left, scratch=scratch
    )


def row_copies(rows_refs, held_rows, landed):
    rows, depth = rows_refs[0].shape
    return [
        pltpu.make_async_copy(
            rows_ref,
            held_rows.at[pl.ds(index % 2 * rows, rows), pl.ds(index // 2 * depth, depth)],
            landed.at[index],
        )
        for index, rows_ref in enumerate(rows_refs)
    ]


def weight_copies(block_ref, start, weight, landed):
    depth, width = weight.shape[0] // 2, weight.shape[1]
    return [
        pltpu.make_async_copy(
            block_ref.at[core, :, pl.ds(start, width)],
            weight.at[pl.ds(core * depth, depth)],
            landed.at[4 + core],
        )
        for core in (0, 1)
    ]


def term_scratch(rows, depth, width):
    return [
        pltpu.VMEM((2 * rows, 2 * depth), jnp.bfloat16),
        pltpu.VMEM((2 * depth, width), jnp.bfloat16),
        pltpu.SemaphoreType.DMA((6,)),
    ]


def held(arrays, earlier, cost=0):
    return pl.pallas_call(
        lambda *refs: None,
        out_shape=[jax.ShapeDtypeStruct(array.shape, array.dtype) for array in arrays],
        in_specs=[LATER] * (len(arrays) + len(earlier)),
        out_specs=[LATER] * len(arrays),
        input_output_aliases={index: index for index in range(len(arrays))},
        cost_estimate=pl.CostEstimate(flops=cost, bytes_accessed=0, transcendentals=0),
        name="held",
    )(*arrays, *earlier)


def gated(gate_scale, parts, video, starts, shape, before=()):
    rows, width = shape[0], shape[1] // 2

    def kernel(video_ref, gate_ref, *refs):
        part_refs = list(refs[: sum(len(half) for part in parts for half in part)])
        out_ref, *held_refs, landed = refs[len(part_refs) + len(before) :]
        halves = video_ref[0] * width, (1 - video_ref[0]) * width
        copies = []
        for part, start in zip(parts, starts):
            for half_start, half in zip(halves, part):
                total = f32(part_refs.pop(0)[...])
                for _ in half[1:]:
                    total = total + f32(part_refs.pop(0)[...])
                columns = pl.ds(pl.multiple_of(half_start + start, TILE), total.shape[1])
                held_ref = held_refs[len(copies)]
                held_ref[...] = (gate_ref[:, columns] * total).astype(held_ref.dtype)
                copies.append(
                    pltpu.make_async_copy(held_ref, out_ref.at[:, columns], landed.at[len(copies)])
                )
                copies[-1].start()
        for copy in copies:
            copy.wait()

    arrays = [array for part in parts for half in part for array in half]
    arrays = (jnp.int32(video).reshape(1), gate_scale.reshape(1, -1), *arrays)
    return pl.pallas_call(
        kernel,
        out_shape=jax.ShapeDtypeStruct(shape, jnp.bfloat16),
        in_specs=[SMEM] + [WHOLE] * (len(arrays) - 1) + [LATER] * len(before),
        out_specs=LATER,
        scratch_shapes=[
            pltpu.VMEM((rows, half[0].shape[1]), jnp.bfloat16) for part in parts for half in part
        ]
        + [pltpu.SemaphoreType.DMA((2 * len(parts),))],
        input_output_aliases={len(arrays): 0} if before else {},
        compiler_params=pltpu.CompilerParams(vmem_limit_bytes=16 * 2**20),
        name="gated",
    )(*arrays, *before)


def square_mesh(queries, key_rows, value_rows, keep_tiles, out_weight, gate_scale):
    video = lax.axis_index("groups")
    slab = lax.axis_index("tm")
    head = lax.axis_index("head")
    width = out_weight.shape[1] // 2
    starts = [width * place // 5 // TILE * TILE for place in STARTS]
    spans = list(zip(starts, starts[1:] + [width]))
    rows = queries.shape[0]
    role = (slab ^ head) & 1
    first = slab // 2 == head // 2

    def passed(array, slab_mask, head_mask, odd):
        pairs = [
            (4 * t + h, 4 * (t ^ slab_mask) + (h ^ head_mask))
            for t in range(4)
            for h in range(4)
            if (t ^ h) & 1 == odd
        ]
        return lax.ppermute(array, ("tm", "head"), pairs)

    lower, upper = halo(key_rows, value_rows)
    half = lax.dynamic_slice_in_dim(out_weight, video * width, width, 1)
    both = jnp.stack([half, passed(half, 0, 1, 1)])
    both, *block_0 = lax.optimization_barrier(
        (both, *[both[..., start:end] for start, end in spans], lower[-1][0], upper[0][0])
    )[: len(spans) + 1]
    block_2 = [passed(part, 2, 0, 0) for part in block_0]
    block_1 = passed(both, 1, 0, 0)

    key_slabs, value_slabs = all_slabs(lower, (key_rows, value_rows), upper)
    mine = attend(queries, key_slabs, value_slabs, keep_tiles)
    to_core, block_1 = lax.optimization_barrier((mine, block_1))
    other = swapped(mine, "groups", 1)
    mine_core = held([swapped(to_core, "head", 1)], [], 100 * 2**33)[0]
    rows_of = (mine, other), (mine_core, swapped(after(other, mine_core), "head", 1))
    block_2[1:] = [held([block], [], 100 * 2**33)[0] for block in block_2[1:]]
    block_3 = [passed(block, 1, 0, 0) for block in block_2]
    block_3[0] = held([block_3[0]], [], 100 * 2**33)[0]
    parts = [
        [(block_0[i], 0), (block_1, spans[i][0]), (block_2[i], 0), (block_3[i], 0)]
        for i in range(len(spans))
    ]

    cost = 100 * 2**33
    summed = []
    early = early_terms(rows_of, parts[-1][:2], role, 0)
    given = [early]
    for part in parts:
        if len(summed) < len(parts) - 1:
            near, far, near_given, far_given = terms(rows_of, part, role, first, cost, given)
            given = [near_given]
        else:
            near, far, near_given, far_given = late_terms(
                rows_of, part[2:], role, first, early, cost, given
            )
        arrived = [swapped(near_given, "head", 2), swapped(far, "groups", 1), diagonal(far_given)]
        if len(summed) < len(parts) - 1:
            arrived = held(arrived, [], 100 * 2**33)
        summed.append(((near, arrived[0]), arrived[1:]))
    out = ()
    for part, (start, _) in zip(summed, spans):
        out = (gated(gate_scale, [part], video, [start], (rows, 2 * width), out),)
    return out[0]


def solution(mesh):
    placed = (
        P(("groups", "tm"), "head", None),
        P(("groups", "tm"), "head", None),
        P(("groups", "tm"), "head", None),
        P(("groups", "tm"), None),
        P("head", "tm"),
        P(("groups", "head")),
    )
    sizes = (mesh.shape["groups"], mesh.shape["tm"], mesh.shape["head"])
    return jax.shard_map(
        square_mesh if sizes == (2, 4, 4) else any_mesh,
        mesh=mesh,
        in_specs=placed,
        out_specs=P(("groups", "tm"), "head"),
        check_vma=False,
    )
```

```python
import functools
import math

import jax
import jax.numpy as jnp
from jax import lax
from jax.experimental import pallas as pl
from jax.experimental.pallas import tpu as pltpu
from jax.sharding import PartitionSpec as P

TILE = 128
STARTS = 0, 2


def passed_along(array, axis, by):
    count = lax.axis_size(axis)
    return lax.ppermute(array, axis, [(i, (i + by) % count) for i in range(count)])


def swapped(array, axis, mask):
    count = lax.axis_size(axis)
    return lax.ppermute(array, axis, [(i, i ^ mask) for i in range(count)])


def attend_kernel(reach, score_scale, keep_ref, queries_ref, *refs):
    key_refs, value_refs, out_ref = refs[: 2 * reach + 1], refs[2 * reach + 1 : -1], refs[-1]
    tiles = queries_ref.shape[1] // TILE
    scale = score_scale * math.log2(math.e)
    for tile in range(tiles):
        query_tile = queries_ref[0, tile * TILE : (tile + 1) * TILE]
        scores = []
        for slab, key_ref in enumerate(key_refs):
            raw = lax.dot_general(
                query_tile, key_ref[0], (((1,), (1,)), ((), ())), preferred_element_type=jnp.float32
            )
            keep = keep_ref[tile : tile + 1, slab * tiles * TILE : (slab + 1) * tiles * TILE]
            scores.append(jnp.where(keep > 0, raw, -jnp.inf))
        peak = scores[0].max(axis=1, keepdims=True)
        for block in scores[1:]:
            peak = jnp.maximum(peak, block.max(axis=1, keepdims=True))
        total, out = 0.0, 0.0
        for block, value_ref in zip(scores, value_refs):
            weights = jnp.exp2((block - peak) * scale)
            total = total + weights.sum(axis=1, keepdims=True)
            out = out + jnp.dot(
                weights.astype(jnp.bfloat16), value_ref[0], preferred_element_type=jnp.float32
            )
        out_ref[tile * TILE : (tile + 1) * TILE] = (out / total).astype(out_ref.dtype)


def attend(queries, key_slabs, value_slabs, keep_tiles):
    rows, head_count, depth = queries.shape
    by_head = [rows_of.transpose(1, 0, 2) for rows_of in (queries, *key_slabs, *value_slabs)]
    keep = jnp.repeat(keep_tiles.astype(jnp.float32), TILE, axis=1)
    block = pl.BlockSpec((1, rows, depth), lambda head: (head, 0, 0))
    return pl.pallas_call(
        functools.partial(attend_kernel, len(key_slabs) // 2, 1.0 / math.sqrt(depth)),
        grid=(head_count,),
        out_shape=jax.ShapeDtypeStruct((rows, head_count * depth), jnp.bfloat16),
        in_specs=[pl.BlockSpec(keep.shape, lambda head: (0, 0))] + [block] * len(by_head),
        out_specs=pl.BlockSpec((rows, depth), lambda head: (0, head)),
        compiler_params=pltpu.CompilerParams(vmem_limit_bytes=16 * 2**20),
        cost_estimate=pl.CostEstimate(flops=2 * 10**10, bytes_accessed=10**7, transcendentals=0),
        name="attend",
    )(keep, *by_head)


def halo(key_rows, value_rows):
    reach_slabs = min(2, (lax.axis_size("tm") - 1) // 2)
    lower_list = []
    upper_list = []
    for distance in range(1, reach_slabs + 1):
        lower_list.append([passed_along(rows, "tm", distance) for rows in (key_rows, value_rows)])
        upper_list.append([passed_along(rows, "tm", -distance) for rows in (key_rows, value_rows)])
    return lower_list[::-1], upper_list


def diagonal(array):
    pairs = [(4 * g + h, 4 * (g ^ 1) + (h ^ 2)) for g in range(2) for h in range(4)]
    return lax.ppermute(array, ("groups", "head"), pairs)


def all_slabs(lower, own, upper):
    ordered = lower + [own] + upper
    return [[slab[which] for slab in ordered] for which in (0, 1)]


def any_mesh(queries, key_rows, value_rows, keep_tiles, out_weight, gate_scale):
    lower, upper = halo(key_rows, value_rows)
    key_slabs, value_slabs = all_slabs(lower, (key_rows, value_rows), upper)
    attended = attend(queries, key_slabs, value_slabs, keep_tiles)
    partial_value = jnp.dot(
        attended,
        lax.all_gather(out_weight, "tm", axis=1, tiled=True),
        preferred_element_type=jnp.float32,
    )
    summed = lax.psum_scatter(
        partial_value.astype(jnp.bfloat16), "head", scatter_dimension=1, tiled=True
    ).astype(jnp.float32)
    return (gate_scale[None, :] * summed).astype(jnp.bfloat16)


def after(array, *others):
    return lax.optimization_barrier((array, *others))[0]


def f32(array):
    return array.astype(jnp.float32)


SMEM = pl.BlockSpec(memory_space=pltpu.SMEM)
WHOLE = pl.BlockSpec(memory_space=pltpu.VMEM)
LATER = pl.BlockSpec(memory_space=pl.ANY)


def local_call(kernel, outs, flags, arrays, earlier, name, flops=0, left=(), scratch=()):
    def body(*refs):
        count = len(flags) + len(arrays) + len(left)
        kernel(*refs[:count], *refs[count + len(earlier) :])

    moved = sum(array.size * array.dtype.itemsize for array in (*arrays, *left, *outs))
    return pl.pallas_call(
        body,
        out_shape=outs,
        in_specs=[SMEM] * len(flags)
        + [WHOLE] * len(arrays)
        + [LATER] * (len(left) + len(earlier)),
        out_specs=[WHOLE] * len(outs),
        scratch_shapes=scratch,
        compiler_params=pltpu.CompilerParams(vmem_limit_bytes=16 * 2**20),
        cost_estimate=pl.CostEstimate(flops=flops, bytes_accessed=moved, transcendentals=0),
        name=name,
    )(*[jnp.int32(flag).reshape(1) for flag in flags], *arrays, *left, *earlier)


def terms(rows_of, blocks, role, first, cost, earlier=()):
    rows, depth = rows_of[0][0].shape
    width = blocks[0][0].shape[2]
    starts = [column for _, column in blocks]
    blocks = [block for block, _ in blocks]
    flat = [array for core in rows_of for array in core]

    def kernel(role_ref, first_ref, *refs):
        rows_refs, block_refs = refs[:4], refs[4:8]
        near_ref, far_ref, near_given_ref, far_given_ref, held_rows, weight, landed = refs[8:]
        out_refs = ((near_ref, far_ref), (near_given_ref, far_given_ref))

        def weight_copies(slot, index):
            return [
                pltpu.make_async_copy(
                    block_refs[index].at[core, :, pl.ds(starts[index], width)],
                    weight.at[slot, pl.ds(core * depth, depth)],
                    landed.at[4 + 2 * slot + core],
                )
                for core in (0, 1)
            ]

        def start_weights(odd, second):
            for slot in (1, 0):
                for copy in weight_copies(slot, odd + 2 * (slot ^ second)):
                    copy.start()

        for odd in (0, 1):
            for second in (0, 1):
                chosen = (role_ref[0] == odd) & (first_ref[0] == 1 - second)
                pl.when(chosen)(functools.partial(start_weights, odd, second))
        rows_copies = [
            pltpu.make_async_copy(
                rows_ref,
                held_rows.at[pl.ds(index % 2 * rows, rows), pl.ds(index // 2 * depth, depth)],
                landed.at[index],
            )
            for index, rows_ref in enumerate(rows_refs)
        ]
        for copy in rows_copies:
            copy.start()
        for copy in rows_copies:
            copy.wait()
        for slot in (1, 0):
            for copy in weight_copies(slot, 0):
                copy.wait()
            total = jnp.dot(held_rows[...], weight[slot], preferred_element_type=jnp.float32)
            for video, out_ref in enumerate(out_refs[slot]):
                out_ref[...] = total[video * rows : (video + 1) * rows].astype(out_ref.dtype)

    kinds = (jnp.float32, jnp.bfloat16, jnp.bfloat16, jnp.bfloat16)
    outs = [jax.ShapeDtypeStruct((rows, width), kind) for kind in kinds]
    scratch = [
        pltpu.VMEM((2 * rows, 2 * depth), jnp.bfloat16),
        pltpu.VMEM((2, 2 * depth, width), jnp.bfloat16),
        pltpu.SemaphoreType.DMA((8,)),
    ]
    left = (*flat, *blocks)
    return local_call(
        kernel, outs, (role, first), (), earlier, "terms", cost, left=left, scratch=scratch
    )


def early_terms(rows_of, blocks, role, cost):
    rows, depth = rows_of[0][0].shape
    width = blocks[0][0].shape[2]
    starts = [column for _, column in blocks]
    flat = [array for core in rows_of for array in core]

    def kernel(role_ref, *refs):
        rows_refs, block_refs, out_ref = refs[:4], refs[4:6], refs[6]
        held_rows, weight, landed = refs[7:]
        copies = row_copies(rows_refs, held_rows, landed)
        for odd in (0, 1):
            for copy in weight_copies(block_refs[odd], starts[odd], weight, landed):
                pl.when(role_ref[0] == odd)(copy.start)
        for copy in copies:
            copy.start()
        for copy in copies + weight_copies(block_refs[0], starts[0], weight, landed):
            copy.wait()
        total = jnp.dot(held_rows[...], weight[...], preferred_element_type=jnp.float32)
        for video in (0, 1):
            out_ref[video] = total[video * rows : (video + 1) * rows]

    out = jax.ShapeDtypeStruct((2, rows, width), jnp.float32)
    left = (*flat, *[block for block, _ in blocks])
    scratch = term_scratch(rows, depth, width)
    return local_call(
        kernel, [out], (role,), (), (), "early_terms", cost, left=left, scratch=scratch
    )[0]


def late_terms(rows_of, blocks, role, first, early, cost, earlier=()):
    rows, depth = rows_of[0][0].shape
    width = blocks[0][0].shape[2]
    starts = [column for _, column in blocks]
    flat = [array for core in rows_of for array in core]

    def kernel(role_ref, first_ref, early_ref, *refs):
        rows_refs, block_refs = refs[:4], refs[4:6]
        near_ref, far_ref, near_given_ref, far_given_ref, held_rows, weight, landed = refs[6:]
        copies = row_copies(rows_refs, held_rows, landed)
        for odd in (0, 1):
            for copy in weight_copies(block_refs[odd], starts[odd], weight, landed):
                pl.when(role_ref[0] == odd)(copy.start)
        for copy in copies:
            copy.start()
        kept_refs, given_refs = (near_ref, far_ref), (near_given_ref, far_given_ref)
        for stays, early_refs in ((1, kept_refs), (0, given_refs)):

            @pl.when(first_ref[0] == stays)
            def _():
                for video in (0, 1):
                    early_refs[video][...] = early_ref[video].astype(early_refs[video].dtype)

        for copy in copies + weight_copies(block_refs[0], starts[0], weight, landed):
            copy.wait()
        total = jnp.dot(held_rows[...], weight[...], preferred_element_type=jnp.float32)
        for stays, late_refs in ((1, given_refs), (0, kept_refs)):

            @pl.when(first_ref[0] == stays)
            def _():
                for video in (0, 1):
                    late = total[video * rows : (video + 1) * rows]
                    late_refs[video][...] = late.astype(late_refs[video].dtype)

    kinds = (jnp.float32, jnp.bfloat16, jnp.bfloat16, jnp.bfloat16)
    outs = [jax.ShapeDtypeStruct((rows, width), kind) for kind in kinds]
    left = (*flat, *[block for block, _ in blocks])
    scratch = term_scratch(rows, depth, width)
    return local_call(
        kernel, outs, (role, first), (early,), earlier, "late_terms", cost, left=left, scratch=scratch
    )


def row_copies(rows_refs, held_rows, landed):
    rows, depth = rows_refs[0].shape
    return [
        pltpu.make_async_copy(
            rows_ref,
            held_rows.at[pl.ds(index % 2 * rows, rows), pl.ds(index // 2 * depth, depth)],
            landed.at[index],
        )
        for index, rows_ref in enumerate(rows_refs)
    ]


def weight_copies(block_ref, start, weight, landed):
    depth, width = weight.shape[0] // 2, weight.shape[1]
    return [
        pltpu.make_async_copy(
            block_ref.at[core, :, pl.ds(start, width)],
            weight.at[pl.ds(core * depth, depth)],
            landed.at[4 + core],
        )
        for core in (0, 1)
    ]


def term_scratch(rows, depth, width):
    return [
        pltpu.VMEM((2 * rows, 2 * depth), jnp.bfloat16),
        pltpu.VMEM((2 * depth, width), jnp.bfloat16),
        pltpu.SemaphoreType.DMA((6,)),
    ]


def held(arrays, earlier, cost=0):
    return pl.pallas_call(
        lambda *refs: None,
        out_shape=[jax.ShapeDtypeStruct(array.shape, array.dtype) for array in arrays],
        in_specs=[LATER] * (len(arrays) + len(earlier)),
        out_specs=[LATER] * len(arrays),
        input_output_aliases={index: index for index in range(len(arrays))},
        cost_estimate=pl.CostEstimate(flops=cost, bytes_accessed=0, transcendentals=0),
        name="held",
    )(*arrays, *earlier)


def gated(gate_scale, parts, video, starts, shape, before=()):
    rows, width = shape[0], shape[1] // 2

    def kernel(video_ref, gate_ref, *refs):
        part_refs = list(refs[: sum(len(half) for part in parts for half in part)])
        out_ref, *held_refs, landed = refs[len(part_refs) + len(before) :]
        halves = video_ref[0] * width, (1 - video_ref[0]) * width
        copies = []
        for part, start in zip(parts, starts):
            for half_start, half in zip(halves, part):
                total = f32(part_refs.pop(0)[...])
                for _ in half[1:]:
                    total = total + f32(part_refs.pop(0)[...])
                columns = pl.ds(pl.multiple_of(half_start + start, TILE), total.shape[1])
                held_ref = held_refs[len(copies)]
                held_ref[...] = (gate_ref[:, columns] * total).astype(held_ref.dtype)
                copies.append(
                    pltpu.make_async_copy(held_ref, out_ref.at[:, columns], landed.at[len(copies)])
                )
                copies[-1].start()
        for copy in copies:
            copy.wait()

    arrays = [array for part in parts for half in part for array in half]
    arrays = (jnp.int32(video).reshape(1), gate_scale.reshape(1, -1), *arrays)
    return pl.pallas_call(
        kernel,
        out_shape=jax.ShapeDtypeStruct(shape, jnp.bfloat16),
        in_specs=[SMEM] + [WHOLE] * (len(arrays) - 1) + [LATER] * len(before),
        out_specs=LATER,
        scratch_shapes=[
            pltpu.VMEM((rows, half[0].shape[1]), jnp.bfloat16) for part in parts for half in part
        ]
        + [pltpu.SemaphoreType.DMA((2 * len(parts),))],
        input_output_aliases={len(arrays): 0} if before else {},
        compiler_params=pltpu.CompilerParams(vmem_limit_bytes=16 * 2**20),
        name="gated",
    )(*arrays, *before)


def square_mesh(queries, key_rows, value_rows, keep_tiles, out_weight, gate_scale):
    video = lax.axis_index("groups")
    slab = lax.axis_index("tm")
    head = lax.axis_index("head")
    width = out_weight.shape[1] // 2
    starts = [width * place // 5 // TILE * TILE for place in STARTS]
    spans = list(zip(starts, starts[1:] + [width]))
    rows = queries.shape[0]
    role = (slab ^ head) & 1
    first = slab // 2 == head // 2

    def passed(array, slab_mask, head_mask, odd):
        pairs = [
            (4 * t + h, 4 * (t ^ slab_mask) + (h ^ head_mask))
            for t in range(4)
            for h in range(4)
            if (t ^ h) & 1 == odd
        ]
        return lax.ppermute(array, ("tm", "head"), pairs)

    lower, upper = halo(key_rows, value_rows)
    half = lax.dynamic_slice_in_dim(out_weight, video * width, width, 1)
    both = jnp.stack([half, passed(half, 0, 1, 1)])
    both, *block_0 = lax.optimization_barrier(
        (both, *[both[..., start:end] for start, end in spans], lower[-1][0], upper[0][0])
    )[: len(spans) + 1]
    block_2 = [passed(part, 2, 0, 0) for part in block_0]
    block_1 = passed(both, 1, 0, 0)

    key_slabs, value_slabs = all_slabs(lower, (key_rows, value_rows), upper)
    mine = attend(queries, key_slabs, value_slabs, keep_tiles)
    to_core, block_1 = lax.optimization_barrier((mine, block_1))
    other = swapped(mine, "groups", 1)
    mine_core = held([swapped(to_core, "head", 1)], [], 100 * 2**33)[0]
    rows_of = (mine, other), (mine_core, swapped(after(other, mine_core), "head", 1))
    block_2[1:] = [held([block], [], 100 * 2**33)[0] for block in block_2[1:]]
    block_3 = [passed(block, 1, 0, 0) for block in block_2]
    block_3[0] = held([block_3[0]], [], 100 * 2**33)[0]
    parts = [
        [(block_0[i], 0), (block_1, spans[i][0]), (block_2[i], 0), (block_3[i], 0)]
        for i in range(len(spans))
    ]

    cost = 100 * 2**33
    summed = []
    early = early_terms(rows_of, parts[-1][:2], role, 0)
    given = [early]
    for part in parts:
        if len(summed) < len(parts) - 1:
            near, far, near_given, far_given = terms(rows_of, part, role, first, cost, given)
            given = [near_given]
        else:
            near, far, near_given, far_given = late_terms(
                rows_of, part[2:], role, first, early, cost, given
            )
        arrived = [swapped(near_given, "head", 2), swapped(far, "groups", 1), diagonal(far_given)]
        if len(summed) < len(parts) - 1:
            arrived = held(arrived, [], 100 * 2**33)
        summed.append(((near, arrived[0]), arrived[1:]))
    out = ()
    for part, (start, _) in zip(summed, spans):
        out = (gated(gate_scale, [part], video, [start], (rows, 2 * width), out),)
    return out[0]


def solution(mesh):
    placed = (
        P(("groups", "tm"), "head", None),
        P(("groups", "tm"), "head", None),
        P(("groups", "tm"), "head", None),
        P(("groups", "tm"), None),
        P("head", "tm"),
        P(("groups", "head")),
    )
    sizes = (mesh.shape["groups"], mesh.shape["tm"], mesh.shape["head"])
    return jax.shard_map(
        square_mesh if sizes == (2, 4, 4) else any_mesh,
        mesh=mesh,
        in_specs=placed,
        out_specs=P(("groups", "tm"), "head"),
        check_vma=False,
    )
```
